256 devices in a mesh: sub: 64 (over z, x, core), crs: 4 (over y).
Axes of the slice: x: 4, y: 4, z: 8, core: 2. Of those that a mesh axis runs over, the one named last changes fastest.
Arguments:
- right_sides: bfloat16 [64, 2304, 512], P('sub'), may hold values from -40 to 40
- stiffness_shift: float32 [64, 2304], P('sub'), may hold values from 0.5 to 8
- local_inverses: bfloat16 [64, 2304, 2304], P('sub', 'crs'), may hold values from -0.5 to 0.5
- eigen_basis: bfloat16 [64, 32, 2304], P('sub'), may hold values from -0.125 to 0.125
- eigen_counts: int32 [64], P('sub'), may hold values from 16 to 32, as said below
- face_indices: int32 [64, 2, 576], P('sub'), may hold values from 0 to 2303, as said below
- coarse_inverse: bfloat16 [2048, 2048], P('crs'), may hold values from -2 to 2
Outputs:
- solution: bfloat16 [64, 2304, 512], P('sub')
- residual_estimate: float32 [512], replicated
The draws below stay inside these ranges and needn't reach their ends.
Inputs may be any that keep to these rules, and one draw needn't show every extreme that they name: `eigen_counts`: some subdomain keeps 32. `face_indices`: the 1152 indices of one subdomain are distinct.
All inputs are finite; a program needn't handle non-finite values.
Results may differ from the reference program's by a relative error of at most 0.006.
Values may be sent and summed in bfloat16 or wider, within the bound.
A program may use at most 128 MiB of HBM per device.

```python
import math
import jax
import jax.numpy as jnp
from jax import lax

NRHS = 512
KMAX = 32
NLOC = 2304
FACE = 576
SUBS = 64
COARSE = 2048


def draw_right_sides(key, part):
    key = jax.random.fold_in(key, 11)
    streams = jax.random.split(key, 3)
    extent = (SUBS, NLOC, NRHS)
    values_raw = jnp.clip(jax.random.normal(streams[0], extent, jnp.float32), -4.0, 4.0)
    growth = 1.0 + 2.0 * jnp.arange(SUBS, dtype=jnp.float32) / float(max(SUBS - 1, 1))
    row_scale = jnp.exp(jax.random.uniform(streams[1], (SUBS, NLOC, 1), jnp.float32, 0.0, 1.1513))
    column_scale = jnp.exp(jax.random.uniform(streams[2], (1, 1, NRHS), jnp.float32, 0.0, 1.1513))
    return (0.3 * values_raw * growth[:, None, None] * row_scale * column_scale).astype(jnp.bfloat16)


def draw_local_inverses(key, part):
    key = jax.random.fold_in(key, 23)
    streams = jax.random.split(key, 2)
    extent = (SUBS, NLOC, NLOC)
    spread_vals = jnp.clip(jax.random.normal(streams[0], extent, jnp.float32), -4.0, 4.0)
    diagonal_vals = jax.random.uniform(streams[1], (SUBS, NLOC, 1), jnp.float32, 0.1, 0.25)
    identity = (lax.broadcasted_iota(jnp.int32, (NLOC, NLOC), 0) == lax.broadcasted_iota(jnp.int32, (NLOC, NLOC), 1)).astype(jnp.float32)
    return (spread_vals * (0.06 / math.sqrt(NLOC)) + identity[None] * diagonal_vals).astype(jnp.bfloat16)


def draw_coarse_inverse(key, part):
    key = jax.random.fold_in(key, 37)
    streams = jax.random.split(key, 2)
    extent = (COARSE, COARSE)
    spread_vals = jnp.clip(jax.random.normal(streams[0], extent, jnp.float32), -4.0, 4.0)
    diagonal_vals = jax.random.uniform(streams[1], (COARSE, 1), jnp.float32, 0.5, 1.5)
    identity = (lax.broadcasted_iota(jnp.int32, extent, 0) == lax.broadcasted_iota(jnp.int32, extent, 1)).astype(jnp.float32)
    return (spread_vals * (0.4 / math.sqrt(COARSE)) + identity * diagonal_vals).astype(jnp.bfloat16)


def draw_eigen_counts(key, part):
    key = jax.random.fold_in(key, 41)
    streams = jax.random.split(key, 2)
    drawn = jax.random.randint(streams[0], (SUBS,), KMAX // 2, KMAX + 1)
    chosen = jax.random.randint(streams[1], (), 0, SUBS)
    return jnp.where(jnp.arange(SUBS, dtype=jnp.int32) == chosen, KMAX, drawn).astype(jnp.int32)


def draw_face_indices(key, part):
    key = jax.random.fold_in(key, 53)
    streams = jax.random.split(key, SUBS)
    orders = jax.vmap(lambda single_key: jax.random.permutation(single_key, NLOC))(streams)
    return orders[:, :2 * FACE].reshape(SUBS, 2, FACE).astype(jnp.int32)


def steps_of(own_key, shape, cuts, smallest, high):
    gain = 1.0
    for axis_at, parts in cuts:
        draws = jax.random.uniform(jax.random.fold_in(jax.random.fold_in(own_key, 6), axis_at), (parts,), jnp.float32, smallest / len(cuts), high / len(cuts))
        gain = gain * jnp.repeat(jnp.exp(draws), shape[axis_at] // parts).reshape((-1,) + (1,) * (len(shape) - 1 - axis_at))
    return gain


def scatter_about(key, dims, scale, bound, pieces=(), kind=jnp.bfloat16):
    loudness = steps_of(key, dims, pieces, -0.22, 0.18) if pieces else 1.0
    values = jax.random.normal(key, dims, jnp.float32) * scale * loudness
    return jnp.minimum(jnp.maximum(values, -bound), bound).astype(kind)


def setup_inputs(seed: int = 0) -> dict:
    key_of = jax.random.split(jax.random.key(seed), 8)
    return {
        "right_sides": draw_right_sides(jax.random.fold_in(key_of[7], 71), 0),
        "stiffness_shift": jnp.clip(jnp.exp(math.log(8.0) - 2.7725887 * jax.random.uniform(key_of[1], (SUBS, NLOC), jnp.float32) ** steps_of(key_of[1], (SUBS, NLOC), ((0, 64),), -0.2, 0.2)), 0.5, 8.0),
        "local_inverses": draw_local_inverses(jax.random.fold_in(key_of[7], 71), 0),
        "eigen_basis": scatter_about(key_of[3], (SUBS, KMAX, NLOC), NLOC ** -0.5, 0.125, ((0, 64),)),
        "eigen_counts": draw_eigen_counts(jax.random.fold_in(key_of[7], 71), 0),
        "face_indices": draw_face_indices(jax.random.fold_in(key_of[7], 71), 0),
        "coarse_inverse": draw_coarse_inverse(jax.random.fold_in(key_of[7], 71), 0),
    }


def apply_operator(vector_in, stiffness_shift, face_indices):
    subs_count, dof_count, width_rhs = vector_in.shape
    component_grid = vector_in.reshape(subs_count, 3, dof_count // 3, width_rhs)
    zero_column = jnp.zeros((subs_count, 3, 1, width_rhs), jnp.float32)
    below_cells = jnp.concatenate([zero_column, component_grid[:, :, :-1]], axis=2)
    above_cells = jnp.concatenate([component_grid[:, :, 1:], zero_column], axis=2)
    cross_terms = lax.optimization_barrier(jnp.sum(component_grid, axis=1, keepdims=True)) - component_grid
    shift_grid = stiffness_shift.reshape(subs_count, 3, dof_count // 3, 1)
    applied = (6.0 + shift_grid) * component_grid - below_cells - above_cells - 0.5 * cross_terms
    applied = applied.reshape(subs_count, dof_count, width_rhs)
    take_rows = jax.vmap(lambda rows_all, picks: rows_all[picks])
    lower_rim = take_rows(vector_in, face_indices[:, 0])
    upper_rim = take_rows(vector_in, face_indices[:, 1])
    zero_rim = jnp.zeros((1,) + lower_rim.shape[1:], jnp.float32)
    from_below = jnp.concatenate([zero_rim, upper_rim[:-1]], axis=0)
    from_above = jnp.concatenate([lower_rim[1:], zero_rim], axis=0)

    def attach(rows_all, lower_picks, upper_picks, below_vals, above_vals):
        return rows_all.at[lower_picks].add(-4.0 * below_vals).at[upper_picks].add(-4.0 * above_vals)
    return jax.vmap(attach)(applied, face_indices[:, 0], face_indices[:, 1], from_below, from_above)

def product_rounded(pair_in):
    return jnp.dot(pair_in[0], pair_in[1], preferred_element_type=jnp.float32).astype(jnp.bfloat16)

def product_back(pair_in):
    return jnp.dot(pair_in[0].T, pair_in[1], preferred_element_type=jnp.float32)

def precondition(vector_in, local_inverses, masked_basis, coarse_inverse):
    vector_half = vector_in.astype(jnp.bfloat16)
    local_whole = lax.map(product_rounded, (local_inverses, vector_half))
    coefficients = lax.map(product_rounded, (masked_basis, vector_half))
    subs_count, basis_width, width_rhs = coefficients.shape
    stacked = coefficients.reshape(subs_count * basis_width, width_rhs)
    coarse_all = jnp.dot(coarse_inverse, stacked, preferred_element_type=jnp.float32).astype(jnp.bfloat16)
    coarse_all = coarse_all.reshape(subs_count, basis_width, width_rhs)
    correction = lax.map(product_back, (masked_basis, coarse_all))
    return local_whole.astype(jnp.float32) + correction

def inner_sum(first_vec, second_vec):
    return lax.optimization_barrier(jnp.sum(first_vec * second_vec, axis=(0, 1)))

def reference(right_sides, stiffness_shift, local_inverses, eigen_basis, eigen_counts, face_indices, coarse_inverse):
    basis_width = eigen_basis.shape[1]
    column_index = jnp.arange(basis_width, dtype=jnp.int32)[None, :, None]
    masked_basis = jnp.where(column_index < eigen_counts[:, None, None], eigen_basis, jnp.zeros_like(eigen_basis))
    source = right_sides.astype(jnp.float32)
    beta = jnp.sqrt(inner_sum(source, source) + 1e-12)
    first = source / beta
    z_one = precondition(first, local_inverses, masked_basis, coarse_inverse)
    w_one = apply_operator(z_one, stiffness_shift, face_indices)
    h11 = inner_sum(w_one, first)
    w_one = w_one - h11 * first
    h21 = jnp.sqrt(inner_sum(w_one, w_one) + 1e-12)
    second = w_one / h21
    z_two = precondition(second, local_inverses, masked_basis, coarse_inverse)
    w_two = apply_operator(z_two, stiffness_shift, face_indices)
    h12 = inner_sum(w_two, first)
    h22 = inner_sum(w_two, second)
    w_two = w_two - h12 * first - h22 * second
    h32 = jnp.sqrt(inner_sum(w_two, w_two) + 1e-12)
    dist_one = jnp.sqrt(h11 * h11 + h21 * h21)
    cos_one = h11 / dist_one
    sin_one = h21 / dist_one
    r12 = cos_one * h12 + sin_one * h22
    t22 = cos_one * h22 - sin_one * h12
    dist_two = jnp.sqrt(t22 * t22 + h32 * h32)
    cos_two = t22 / dist_two
    sin_two = h32 / dist_two
    coef_two = -cos_two * sin_one * beta / dist_two
    coef_one = (cos_one * beta - r12 * coef_two) / dist_one
    solution = (z_one * coef_one + z_two * coef_two).astype(jnp.bfloat16)
    residual_estimate = jnp.abs(sin_one * sin_two)
    return (solution, residual_estimate)
```

```python
import functools

import jax
import jax.numpy as jnp
from jax import lax
from jax.experimental import pallas as pl
from jax.experimental.pallas import tpu as pltpu
from jax.sharding import PartitionSpec as P

MESH = pl.DeviceIdType.MESH
F32 = jnp.float32
BF16 = jnp.bfloat16
LANES = 128
HALF = 256
PAD = 8


def dot(a, b):
    return jnp.dot(a, b, preferred_element_type=F32)


def twice(row_block):
    return jnp.concatenate([row_block, row_block], axis=1)


def tile_of(rows, most, unit):
    tile = unit
    for size in range(unit, most + 1, unit):
        if rows % size == 0:
            tile = size
    return tile


def kernel(
    plan,
    b_hbm,
    inv_hbm,
    cinv_hbm,
    shift_ref,
    basis_ref,
    count_ref,
    face_ref,
    sol_hbm,
    res_ref,
    bv,
    inv,
    crow,
    mbasis,
    mbasis_t,
    wide,
    shift_col,
    pick,
    place,
    local,
    zpad,
    zb,
    ubuf,
    ub16,
    pbuf,
    fsend,
    frecv,
    cg,
    co,
    rb1,
    rb2,
    ssem,
    rsem,
    lsem,
):
    nz, nx, ny = plan
    nj = 2 * nx
    subs = nz * nj
    kmax, n = basis_ref.shape
    cells = n // 3
    nq = n // ny
    hq = nq // 2
    faces = face_ref.shape[1]
    face = faces // 2

    me_s = lax.axis_index("sub")
    me_y = lax.axis_index("crs")
    core = lax.rem(me_s, 2)
    j = lax.rem(me_s, nj)
    x = j // 2
    z = me_s // nj

    def at_y(k):
        return (me_s, lax.rem(me_y + k, ny))

    def at_z(k):
        return (lax.rem(z + k, nz) * nj + j, me_y)

    def at_j(k):
        return (z * nj + lax.rem(j + k, nj), me_y)

    def at_x(k):
        return (z * nj + lax.rem(x + k, nx) * 2 + core, me_y)

    other_core = (me_s + 1 - 2 * core, me_y)
    above = (lax.rem(me_s + 1, subs), me_y)
    below = (lax.rem(me_s + subs - 1, subs), me_y)

    used = [0]
    sent = []

    def remote(src, dst, device, slot=None):
        i = used[0]
        used[0] += 1
        cp = pltpu.make_async_remote_copy(
            src_ref=src,
            dst_ref=dst,
            send_sem=ssem.at[i],
            recv_sem=rsem.at[i],
            device_id=device,
            device_id_type=MESH,
        )
        cp.start()
        sent.append(cp)
        arrived = pltpu.make_async_remote_copy(
            src_ref=src if slot is None else slot,
            dst_ref=dst if slot is None else slot,
            send_sem=ssem.at[i],
            recv_sem=rsem.at[i],
            device_id=device,
            device_id_type=MESH,
        )
        return arrived

    loads = []
    for h in range(2):
        cp = pltpu.make_async_copy(b_hbm.at[:, pl.ds(h * HALF, HALF)], bv.at[h], lsem.at[h])
        cp.start()
        loads.append(cp)
    load_inv = pltpu.make_async_copy(inv_hbm, inv, lsem.at[2])
    load_inv.start()

    barrier = pltpu.get_barrier_semaphore()
    partners = [at_y(k) for k in range(1, ny)] + [at_z(k) for k in range(1, nz)]
    partners += [at_j(k) for k in range(1, nj)] + [above, below]
    for device in partners:
        pl.semaphore_signal(barrier, inc=1, device_id=device, device_id_type=MESH)

    keep = lax.broadcasted_iota(jnp.int32, (kmax, n), 0) < count_ref[0]
    masked = jnp.where(keep, basis_ref[...].astype(F32), 0.0)
    mbasis[...] = masked.astype(BF16)
    wide[...] = jnp.zeros_like(wide)
    wide[pl.ds(0, kmax), :] = masked
    for i in range(n // LANES):
        block = wide[:, i * LANES : (i + 1) * LANES]
        mbasis_t[pl.ds(i * LANES, LANES), :] = block.T.astype(BF16)

    pl.semaphore_wait(barrier, len(partners))

    panel = cinv_hbm.shape[0]
    owner = me_s * kmax // panel
    offset = pl.multiple_of(lax.rem(me_s * kmax, panel), kmax)
    row_sem = used[0]
    used[0] += ny - 1

    def row_copy(k):
        return pltpu.make_async_remote_copy(
            src_ref=cinv_hbm.at[pl.ds(offset, kmax), :],
            dst_ref=crow,
            send_sem=ssem.at[row_sem + k - 1],
            recv_sem=rsem.at[row_sem],
            device_id=at_y(k),
            device_id_type=MESH,
        )

    own_rows = pltpu.make_async_copy(cinv_hbm.at[pl.ds(offset, kmax), :], crow, lsem.at[3])

    @pl.when(me_y == owner)
    def _():
        for k in range(1, ny):
            row_copy(k).start()
        own_rows.start()

    my_half = me_y // 2
    my_side = lax.rem(me_y, 2)

    def coarse_begin(it, field):
        part = dot(mbasis[...], field[my_half])
        own = jnp.where(my_side == 0, part[:, :LANES], part[:, LANES:])
        cg[it, z, x, core] = own.astype(BF16)
        waits = []
        for k in range(1, nz):
            mine = cg.at[it, z, x, core]
            waits.append(remote(mine, mine, at_z(k), cg.at[it, lax.rem(z + nz - k, nz), x, core]))
        return waits

    def coarse_x(it, waits):
        for w in waits:
            w.wait_recv()
        out = []
        for k in range(1, nx):
            mine = cg.at[it, :, x, core]
            out.append(remote(mine, mine, at_x(k), cg.at[it, :, lax.rem(x + nx - k, nx), core]))
        return out

    def coarse_core(it, waits):
        for w in waits:
            w.wait_recv()
        mine = cg.at[it, :, :, core]
        return remote(mine, mine, other_core, cg.at[it, :, :, 1 - core])

    def coarse_end(it, wait):
        wait.wait_recv()
        stacked = cg[it].reshape(subs * kmax, LANES)
        co[it, me_y] = dot(crow[...], stacked).astype(BF16)
        waits = []
        for k in range(1, ny):
            mine = co.at[it, me_y]
            waits.append(remote(mine, mine, at_y(k), co.at[it, lax.rem(me_y + ny - k, ny)]))
        return waits

    base = pl.multiple_of(me_y * nq, nq)
    right, left = at_y(1), at_y(ny - 1)

    def part_rows(k, low):
        owner_y = lax.rem(me_y + k, ny)
        return pl.ds(pl.multiple_of(owner_y * nq + (0 if low else hq), hq), hq)

    def local_product(it, h, field):
        tile = tile_of(nq, 288, 16)

        @pl.loop(0, nq // tile)
        def _(i):
            rows = pl.ds(pl.multiple_of(i * tile, tile), tile)
            out = dot(inv[rows, :], field[h])
            local[it, h, pl.ds(pl.multiple_of(base + i * tile, 16), tile), :] = out.astype(BF16)

    def gather_begin(it, h):
        buf = local.at[it, h]

        def send(k, low, device):
            mine = buf.at[part_rows(0, low), :]
            return remote(mine, mine, device, buf.at[part_rows(k, low), :])

        from_left_low = send(ny - 1, True, right)
        from_right_high = send(1, False, left)
        from_left_high = send(ny - 1, False, right)
        from_right_low = send(1, True, left)
        return from_left_low, from_right_high, from_left_high, from_right_low

    def gather_forward(it, h, waits):
        buf = local.at[it, h]
        waits[0].wait_recv()
        low = buf.at[part_rows(ny - 1, True), :]
        far_low = remote(low, low, right, buf.at[part_rows(2, True), :])
        waits[1].wait_recv()
        high = buf.at[part_rows(1, False), :]
        far_high = remote(high, high, left, buf.at[part_rows(2, False), :])
        return waits[2], waits[3], far_low, far_high

    def assemble(it, h):
        top = jnp.concatenate([co[it, 2 * h], co[it, 2 * h + 1]], axis=1)
        coarse = jnp.concatenate([top, jnp.zeros((LANES - kmax, HALF), BF16)], axis=0)
        tile = tile_of(cells, 256, 16)
        per = cells // tile

        @pl.loop(0, 3 * per)
        def _(i):
            comp = i // per
            rows = pl.ds(pl.multiple_of(i * tile, tile), tile)
            value = local[it, h, rows, :].astype(F32) + dot(mbasis_t[rows, :], coarse)
            start = pl.multiple_of(lax.rem(i, per) * tile + PAD, PAD)
            zpad[it, h, comp, pl.ds(start, tile), :] = value
            zb[rows, :] = value.astype(BF16)

    def faces_begin(it, h):
        tile = tile_of(faces, 288, 16)

        @pl.loop(0, faces // tile)
        def _(i):
            rows = pl.ds(pl.multiple_of(i * tile, tile), tile)
            fsend[it, h, rows, :] = dot(pick[rows, :], zb[...]).astype(BF16)

        lower, upper = pl.ds(0, face), pl.ds(face, face)
        from_below = remote(
            fsend.at[it, h, upper, :], frecv.at[it, h, lower, :], above, frecv.at[it, h, lower, :]
        )
        from_above = remote(
            fsend.at[it, h, lower, :], frecv.at[it, h, upper, :], below, frecv.at[it, h, upper, :]
        )
        return from_below, from_above

    def stencil(it, h, waits, h11):
        for w in waits:
            w.wait_recv()
        tile = tile_of(n, 256, 16)

        @pl.loop(0, n // tile)
        def _(i):
            rows = pl.ds(pl.multiple_of(i * tile, tile), tile)
            pbuf[rows, :] = dot(place[rows, :], frecv[it, h])

        size = tile_of(cells, 32, 16)

        def fold(value):
            return jnp.sum(value.reshape(size // 8, 8, HALF), axis=0)

        def step(i, sums):
            m0 = pl.multiple_of(i * size, size)
            blocks = [
                zpad[it, h, comp, pl.ds(m0, size + 2 * PAD), :] for comp in range(3)
            ]
            mid = [block[PAD : PAD + size] for block in blocks]
            total = mid[0] + mid[1] + mid[2]
            s0, s1, s2 = sums
            for comp in range(3):
                rows = pl.ds(pl.multiple_of(comp * cells + m0, size), size)
                value = (6.5 + twice(shift_col[rows, :])) * mid[comp] - 0.5 * total
                value -= blocks[comp][PAD - 1 : PAD - 1 + size]
                value -= blocks[comp][PAD + 1 : PAD + 1 + size]
                value -= 4.0 * pbuf[rows, :]
                b = bv[h, rows, :].astype(F32)
                if it == 0:
                    ubuf[h, rows, :] = value
                    ub16[h, rows, :] = value.astype(BF16)
                    s0, s1, s2 = s0 + fold(b * b), s1 + fold(value * b), s2 + fold(value * value)
                else:
                    u = ubuf[h, rows, :]
                    g = value - h11 * u
                    t = u - h11 * b
                    s0, s1, s2 = s0 + fold(g * b), s1 + fold(g * t), s2 + fold(g * g)
            return s0, s1, s2

        zero = jnp.zeros((8, HALF), F32)
        sums = lax.fori_loop(0, cells // size, step, (zero, zero, zero))
        rows = []
        for value in sums:
            row = jnp.sum(value, axis=0, keepdims=True)
            rows += [row[:, :LANES], row[:, LANES:]]
        return jnp.concatenate(rows + [jnp.zeros((2, LANES), F32)], axis=0)

    def reduce_begin(it, h, partial):
        rb1[it, h, j] = partial
        mine = rb1.at[it, h, j]
        return [
            remote(mine, mine, at_j(k), rb1.at[it, h, lax.rem(j + nj - k, nj)]) for k in range(1, nj)
        ]

    def reduce_z(it, h, waits):
        for w in waits:
            w.wait_recv()
        rb2[it, h, z] = jnp.sum(rb1[it, h], axis=0)
        mine = rb2.at[it, h, z]
        return [
            remote(mine, mine, at_z(k), rb2.at[it, h, lax.rem(z + nz - k, nz)]) for k in range(1, nz)
        ]

    def reduce_end(it, h, waits):
        for w in waits:
            w.wait_recv()
        total = jnp.sum(rb2[it, h], axis=0)
        return [
            jnp.concatenate([total[2 * i : 2 * i + 1], total[2 * i + 1 : 2 * i + 2]], axis=1)
            for i in range(3)
        ]

    for cp in loads:
        cp.wait()
    coarse_wait = coarse_begin(0, bv)
    load_inv.wait()
    local_product(0, 0, bv)
    g00 = gather_begin(0, 0)
    local_product(0, 1, bv)

    zero_rows = jnp.zeros((PAD, HALF), F32)
    for it in range(2):
        for h in range(2):
            for comp in range(3):
                zpad[it, h, comp, pl.ds(0, PAD), :] = zero_rows
                zpad[it, h, comp, pl.ds(cells + PAD, PAD), :] = zero_rows

    for i in range(n // LANES):
        row = jnp.broadcast_to(shift_ref[:, i * LANES : (i + 1) * LANES], (LANES, LANES))
        shift_col[pl.ds(i * LANES, LANES), :] = row.T

    coarse_wait = coarse_x(0, coarse_wait)

    lane = lax.broadcasted_iota(jnp.int32, (LANES, LANES), 1)
    line = lax.broadcasted_iota(jnp.int32, (LANES, LANES), 0)
    for i in range(faces // LANES):
        row = jnp.broadcast_to(face_ref[:, i * LANES : (i + 1) * LANES], (LANES, LANES))
        column = row.astype(F32).T.astype(jnp.int32)
        for k in range(n // LANES):
            hit = jnp.where(column == lane + k * LANES, 1.0, 0.0)
            pick[pl.ds(i * LANES, LANES), k * LANES : (k + 1) * LANES] = hit.astype(BF16)

    g00 = gather_forward(0, 0, g00)
    g01 = gather_begin(0, 1)
    coarse_wait = coarse_core(0, coarse_wait)

    for i in range(faces // LANES):
        row = jnp.broadcast_to(face_ref[:, i * LANES : (i + 1) * LANES], (LANES, LANES))
        slot = lane + i * LANES
        missing = ((slot < face) & (me_s == 0)) | ((slot >= face) & (me_s == subs - 1))
        row = jnp.where(missing, -1, row)
        for k in range(n // LANES):
            hit = jnp.where(row == line + k * LANES, 1.0, 0.0)
            place[pl.ds(k * LANES, LANES), i * LANES : (i + 1) * LANES] = hit.astype(BF16)

    @pl.when(me_y == owner)
    def _():
        own_rows.wait()
        for k in range(1, ny):
            row_copy(k).wait_send()

    @pl.when(me_y != owner)
    def _():
        row_copy(1).wait_recv()

    coarse_wait = coarse_end(0, coarse_wait)
    for w in coarse_wait:
        w.wait_recv()
    for w in g00:
        w.wait_recv()
    assemble(0, 0)
    f00 = faces_begin(0, 0)
    g01 = gather_forward(0, 1, g01)
    p00 = stencil(0, 0, f00, None)
    r00 = reduce_begin(0, 0, p00)
    local_product(1, 0, ub16)
    g10 = gather_begin(1, 0)
    for w in g01:
        w.wait_recv()
    assemble(0, 1)
    f01 = faces_begin(0, 1)
    g10 = gather_forward(1, 0, g10)
    r00 = reduce_z(0, 0, r00)
    p01 = stencil(0, 1, f01, None)
    r01 = reduce_begin(0, 1, p01)
    coarse_wait = coarse_begin(1, ub16)
    local_product(1, 1, ub16)
    g11 = gather_begin(1, 1)
    r01 = reduce_z(0, 1, r01)
    coarse_wait = coarse_x(1, coarse_wait)
    sums1 = [reduce_end(0, 0, r00), None]
    coarse_wait = coarse_core(1, coarse_wait)
    sums1[1] = reduce_end(0, 1, r01)
    coarse_wait = coarse_end(1, coarse_wait)
    g11 = gather_forward(1, 1, g11)

    scalars = []
    for bb, ub, uu in sums1:
        beta2 = bb + 1e-12
        beta = jnp.sqrt(beta2)
        h11 = ub / beta2
        h21s = jnp.maximum((uu - h11 * (2.0 * ub - h11 * bb)) / beta2, 0.0) + 1e-12
        scalars.append((bb, beta2, beta, h11, h21s, jnp.sqrt(h21s)))

    for w in coarse_wait:
        w.wait_recv()
    for w in g10:
        w.wait_recv()
    assemble(1, 0)
    f10 = faces_begin(1, 0)
    p10 = stencil(1, 0, f10, scalars[0][3])
    r10 = reduce_begin(1, 0, p10)
    for w in g11:
        w.wait_recv()
    assemble(1, 1)
    f11 = faces_begin(1, 1)
    r10 = reduce_z(1, 0, r10)
    p11 = stencil(1, 1, f11, scalars[1][3])
    r11 = reduce_begin(1, 1, p11)

    def finish(h, sums):
        bb, beta2, beta, h11, h21s, h21 = scalars[h]
        gb, gt, gg = sums
        scale = 1.0 / (beta * h21)
        h12 = gb * scale / beta
        h22 = gt * scale * scale
        ww = gg * scale * scale
        ff_gap = 1e-12 / beta2
        ss_gap = 1e-12 / h21s
        fs = h11 * ff_gap / h21
        h32s = ww - h12 * h12 * (1.0 + ff_gap) - h22 * h22 * (1.0 + ss_gap) + 2.0 * h12 * h22 * fs
        h32 = jnp.sqrt(jnp.maximum(h32s, 0.0) + 1e-12)
        dist_one = jnp.sqrt(h11 * h11 + h21 * h21)
        cos_one = h11 / dist_one
        sin_one = h21 / dist_one
        r12 = cos_one * h12 + sin_one * h22
        t22 = cos_one * h22 - sin_one * h12
        dist_two = jnp.sqrt(t22 * t22 + h32 * h32)
        cos_two = t22 / dist_two
        sin_two = h32 / dist_two
        y2 = -cos_two * sin_one * beta / dist_two
        y1 = (cos_one * beta - r12 * y2) / dist_one
        weight_two = y2 * scale
        weight_one = y1 / beta - h11 * weight_two
        res_ref[:, h * HALF : (h + 1) * HALF] = jnp.abs(sin_one * sin_two)
        size = tile_of(cells, 64, 16)
        per = cells // size

        @pl.loop(0, 3 * per)
        def _(i):
            comp = i // per
            start = pl.multiple_of(lax.rem(i, per) * size + PAD, PAD)
            one = zpad[0, h, comp, pl.ds(start, size), :]
            two = zpad[1, h, comp, pl.ds(start, size), :]
            rows = pl.ds(pl.multiple_of(i * size, size), size)
            bv[h, rows, :] = (one * weight_one + two * weight_two).astype(BF16)

        out = pltpu.make_async_copy(bv.at[h], sol_hbm.at[:, pl.ds(h * HALF, HALF)], lsem.at[4 + h])
        out.start()
        return out

    r10 = reduce_end(1, 0, r10)
    out0 = finish(0, r10)
    r11 = reduce_z(1, 1, r11)
    r11 = reduce_end(1, 1, r11)
    out1 = finish(1, r11)
    for cp in sent:
        cp.wait_send()
    out0.wait()
    out1.wait()


def count_copies(nz, nx, ny):
    nj = 2 * nx
    coarse = 2 * ((nz - 1) + (nx - 1) + 1 + (ny - 1))
    return (ny - 1) + coarse + 4 * 6 + 4 * 2 + 4 * ((nj - 1) + (nz - 1))


def per_device(nz, nx, right_sides, shift, inverses, basis, counts, face_rows, coarse_inverse):
    ny = lax.axis_size("crs")
    n, width = right_sides.shape[1:]
    nq = n // ny
    kmax = basis.shape[1]
    faces = 2 * face_rows.shape[2]
    cells = n // 3
    nj = 2 * nx
    subs = nz * nj
    copies = count_copies(nz, nx, ny)
    any_spec = pl.BlockSpec(memory_space=pl.ANY)
    vmem = pl.BlockSpec(memory_space=pltpu.VMEM)
    out, residual = pl.pallas_call(
        functools.partial(kernel, (nz, nx, ny)),
        out_shape=(
            jax.ShapeDtypeStruct((n, width), BF16),
            jax.ShapeDtypeStruct((1, width), F32),
        ),
        in_specs=[
            any_spec,
            any_spec,
            any_spec,
            vmem,
            vmem,
            pl.BlockSpec(memory_space=pltpu.SMEM),
            vmem,
        ],
        out_specs=(any_spec, vmem),
        scratch_shapes=[
            pltpu.VMEM((2, n, HALF), BF16),
            pltpu.VMEM((nq, n), BF16),
            pltpu.VMEM((kmax, subs * kmax), BF16),
            pltpu.VMEM((kmax, n), BF16),
            pltpu.VMEM((n, LANES), BF16),
            pltpu.VMEM((LANES, n), F32),
            pltpu.VMEM((n, LANES), F32),
            pltpu.VMEM((faces, n), BF16),
            pltpu.VMEM((n, faces), BF16),
            pltpu.VMEM((2, 2, n, HALF), BF16),
            pltpu.VMEM((2, 2, 3, cells + 2 * PAD, HALF), F32),
            pltpu.VMEM((n, HALF), BF16),
            pltpu.VMEM((2, n, HALF), F32),
            pltpu.VMEM((2, n, HALF), BF16),
            pltpu.VMEM((n, HALF), F32),
            pltpu.VMEM((2, 2, faces, HALF), BF16),
            pltpu.VMEM((2, 2, faces, HALF), BF16),
            pltpu.VMEM((2, nz, nx, 2, kmax, LANES), BF16),
            pltpu.VMEM((2, ny, kmax, LANES), BF16),
            pltpu.VMEM((2, 2, nj, 8, LANES), F32),
            pltpu.VMEM((2, 2, nz, 8, LANES), F32),
            pltpu.SemaphoreType.DMA((copies,)),
            pltpu.SemaphoreType.DMA((copies,)),
            pltpu.SemaphoreType.DMA((6,)),
        ],
        compiler_params=pltpu.CompilerParams(
            collective_id=0, has_side_effects=True, vmem_limit_bytes=60 * 1024 * 1024
        ),
    )(
        right_sides[0],
        inverses[0],
        coarse_inverse,
        shift,
        basis[0],
        counts,
        face_rows.reshape(1, faces),
    )
    return out[None], residual.reshape(width)


def solution(mesh):
    subs = mesh.shape["sub"]
    nz = 8 if subs == 64 else 2
    nx = subs // (2 * nz)
    return jax.shard_map(
        functools.partial(per_device, nz, nx),
        mesh=mesh,
        in_specs=(
            P("sub", None, None),
            P("sub", None),
            P("sub", "crs", None),
            P("sub", None, None),
            P("sub"),
            P("sub", None, None),
            P("crs", None),
        ),
        out_specs=(P("sub", None, None), P()),
        check_vma=False,
    )
```

```python
import functools

import jax
import jax.numpy as jnp
from jax import lax
from jax.experimental import pallas as pl
from jax.experimental.pallas import tpu as pltpu
from jax.sharding import PartitionSpec as P

MESH = pl.DeviceIdType.MESH
F32 = jnp.float32
BF16 = jnp.bfloat16
LANES = 128
HALF = 256
PAD = 8


def dot(a, b):
    return jnp.dot(a, b, preferred_element_type=F32)


def twice(block):
    return jnp.concatenate([block, block], axis=1)


def tile_of(rows, most, unit):
    tile = unit
    for size in range(unit, most + 1, unit):
        if rows % size == 0:
            tile = size
    return tile


def kernel(
    plan,
    b_hbm,
    inv_hbm,
    cinv_hbm,
    shift_ref,
    basis_ref,
    count_ref,
    face_ref,
    sol_hbm,
    res_ref,
    bv,
    inv,
    basis_t,
    wide,
    shift_col,
    pick,
    place,
    inv_place,
    acc,
    local,
    prio,
    zpad,
    zb,
    ubuf,
    ub16,
    fsend,
    frecv,
    zq,
    zbq,
    yq,
    uq,
    fsend_q,
    frecv_q,
    crows,
    select,
    cpart,
    coef,
    cg,
    cpsend,
    cprecv,
    co,
    rb1,
    rb2,
    weights,
    ssem,
    rsem,
    lsem,
):
    nz, nx, ny = plan
    nj = 2 * nx
    subs = nz * nj
    kmax, n = basis_ref.shape
    cells = n // 3
    nq = n // ny
    hq = nq // 2
    face = face_ref.shape[1]
    faces = 2 * face

    me_s = lax.axis_index("sub")
    me_y = lax.axis_index("crs")
    j = lax.rem(me_s, nj)
    z = me_s // nj
    my_half = me_y // 2
    my_side = lax.rem(me_y, 2)

    def at_y(k):
        return (me_s, lax.rem(me_y + k, ny))

    def at_z(k):
        return (lax.rem(z + k, nz) * nj + j, me_y)

    def at_j(k):
        return (z * nj + lax.rem(j + k, nj), me_y)

    above = (lax.rem(me_s + 1, subs), me_y)
    below = (lax.rem(me_s + subs - 1, subs), me_y)

    def side(block):
        return jnp.where(my_side == 0, block[:, :LANES], block[:, LANES:])

    used = [0]
    sent = []

    def describe(i, src, dst, device):
        return pltpu.make_async_remote_copy(
            src_ref=src,
            dst_ref=dst,
            send_sem=ssem.at[i],
            recv_sem=rsem.at[i],
            device_id=device,
            device_id_type=MESH,
        )

    def remote(src, dst, device, slot):
        i = used[0]
        used[0] += 1
        cp = describe(i, src, dst, device)
        cp.start()
        sent.append(cp)
        arrived = describe(i, slot, slot, device)
        return arrived

    def wait_all(waits):
        for w in waits:
            w.wait_recv()

    ext = nq + kmax
    cut = ext // 2
    tiles = ((0, cut), (cut, ext - cut))

    def load_b(h):
        return pltpu.make_async_copy(b_hbm.at[:, pl.ds(h * HALF, HALF)], bv.at[h], lsem.at[h])

    def load_inv(i):
        rows = pl.ds(tiles[i][0], min(tiles[i][1], nq - tiles[i][0]))
        return pltpu.make_async_copy(inv_hbm.at[rows, :], inv.at[rows, :], lsem.at[2 + i])

    loads = [load_b(0), load_inv(0), load_inv(1), load_b(1)]
    for cp in loads:
        cp.start()

    barrier = pltpu.get_barrier_semaphore()
    partners = [at_y(k) for k in range(1, ny)] + [at_z(k) for k in range(1, nz)]
    partners += [at_j(k) for k in range(1, nj)] + [above, below]
    for device in partners:
        pl.semaphore_signal(barrier, inc=1, device_id=device, device_id_type=MESH)

    panel = cinv_hbm.shape[0]
    line_rows = nj * kmax
    owner = z * line_rows // panel
    offset = pl.multiple_of(lax.rem(z * line_rows, panel), line_rows)
    own_rows = pltpu.make_async_copy(cinv_hbm.at[pl.ds(offset, line_rows), :], crows, lsem.at[4])

    @pl.when(me_y == owner)
    def _():
        own_rows.start()

    keep = lax.broadcasted_iota(jnp.int32, (kmax, n), 0) < count_ref[0]
    masked = jnp.where(keep, basis_ref[...].astype(F32), 0.0)
    inv[pl.ds(nq, kmax), :] = masked.astype(BF16)
    wide[...] = jnp.zeros_like(wide)
    wide[pl.ds(0, kmax), :] = masked

    @pl.when(me_y == owner)
    def _():
        at = lax.broadcasted_iota(jnp.int32, select.shape, 0)
        col = lax.broadcasted_iota(jnp.int32, select.shape, 1)
        wanted = (col // kmax) * line_rows + j * kmax + lax.rem(col, kmax)
        select[...] = jnp.where(at == wanted, 1.0, 0.0).astype(BF16)
        own_rows.wait()
        cpart[...] = dot(crows[...], select[...]).astype(BF16)

    pl.semaphore_wait(barrier, len(partners))

    part_sem = used[0]
    used[0] += ny - 1

    def part_copy(k):
        return pltpu.make_async_remote_copy(
            src_ref=cpart,
            dst_ref=cpart,
            send_sem=ssem.at[part_sem + k - 1],
            recv_sem=rsem.at[part_sem],
            device_id=at_y(k),
            device_id_type=MESH,
        )

    def part_begin():
        @pl.when(me_y == owner)
        def _():
            for k in range(1, ny):
                part_copy(k).start()

    def part_end():
        @pl.when(me_y == owner)
        def _():
            for k in range(1, ny):
                part_copy(k).wait_send()

        @pl.when(me_y != owner)
        def _():
            part_copy(1).wait_recv()

    def coarse_begin(it):
        cg[it, z] = side(coef[it, my_half]).astype(BF16)
        mine = cg.at[it, z]
        return [
            remote(mine, mine, at_z(k), cg.at[it, lax.rem(z + nz - k, nz)]) for k in range(1, nz)
        ]

    def coarse_line(it, waits):
        wait_all(waits)
        partial = dot(cpart[...], cg[it].reshape(nz * kmax, LANES))
        cpsend[it] = partial.reshape(nj, kmax, LANES)
        cprecv[it, j] = cpsend[it, j]
        return [
            remote(
                cpsend.at[it, lax.rem(j + k, nj)],
                cprecv.at[it, j],
                at_j(k),
                cprecv.at[it, lax.rem(j + nj - k, nj)],
            )
            for k in range(1, nj)
        ]

    def coarse_end(it, waits):
        wait_all(waits)
        co[it, me_y] = jnp.sum(cprecv[it], axis=0).astype(BF16)
        mine = co.at[it, me_y]
        return [
            remote(mine, mine, at_y(k), co.at[it, lax.rem(me_y + ny - k, ny)])
            for k in range(1, ny)
        ]

    base = pl.multiple_of(me_y * nq, nq)
    right, left = at_y(1), at_y(ny - 1)

    def part_rows(k, low):
        owner_y = lax.rem(me_y + k, ny)
        return pl.ds(pl.multiple_of(owner_y * nq + (0 if low else hq), hq), hq)

    def keep_product(it, h, start, size, out):
        rows = min(size, nq - start)
        local[it, h, pl.ds(pl.multiple_of(base + start, 16), rows), :] = out[:rows].astype(BF16)
        if rows < size:
            coef[it, h] = out[rows:]

    def first_product(h, ready=None):
        for i, (start, size) in enumerate(tiles):
            if ready is not None:
                ready(i)
            keep_product(0, h, start, size, dot(inv[pl.ds(start, size), :], bv[h]))

    def second_product(h):
        for start, size in tiles:
            acc[pl.ds(start, size), :] = dot(inv[pl.ds(start, size), :], ub16[...])

    def second_faces(h, waits):
        wait_all(waits)
        for start, size in tiles:
            rows = pl.ds(start, size)
            out = acc[rows, :] - 4.0 * dot(inv_place[rows, :], frecv[h])
            keep_product(1, h, start, size, out)

    def gather_begin(it, h, first):
        buf = local.at[it, h]

        def send(k, low, device):
            mine = buf.at[part_rows(0, low), :]
            return remote(mine, mine, device, buf.at[part_rows(k, low), :])

        if first:
            return send(ny - 1, True, right), send(1, False, left)
        return send(ny - 1, False, right), send(1, True, left)

    def gather_forward(it, h, waits):
        buf = local.at[it, h]
        waits[0].wait_recv()
        low = buf.at[part_rows(ny - 1, True), :]
        far_low = remote(low, low, right, buf.at[part_rows(2, True), :])
        waits[1].wait_recv()
        high = buf.at[part_rows(1, False), :]
        far_high = remote(high, high, left, buf.at[part_rows(2, False), :])
        return far_low, far_high

    def padded(block):
        rest = jnp.zeros((LANES - kmax, block.shape[1]), BF16)
        return jnp.concatenate([block, rest], axis=0)

    def coarse_half(it, h):
        return padded(jnp.concatenate([co[it, 2 * h], co[it, 2 * h + 1]], axis=1))

    def assemble(h):
        coarse = coarse_half(0, h)
        tile = tile_of(cells, 768, 16)
        per = cells // tile

        @pl.loop(0, 3 * per)
        def _(i):
            comp = i // per
            rows = pl.ds(pl.multiple_of(i * tile, tile), tile)
            value = local[0, h, rows, :].astype(F32) + dot(basis_t[rows, :], coarse)
            start = pl.multiple_of(lax.rem(i, per) * tile + PAD, PAD)
            zpad[h, comp, pl.ds(start, tile), :] = value
            zb[rows, :] = value.astype(BF16)

    def assemble_quarter(field):
        coarse = padded(co[1, me_y])
        tile = tile_of(cells, 768, 16)
        per = cells // tile

        @pl.loop(0, 3 * per)
        def _(i):
            comp = i // per
            rows = pl.ds(pl.multiple_of(i * tile, tile), tile)
            value = field(rows).astype(F32) + dot(basis_t[rows, :], coarse)
            start = pl.multiple_of(lax.rem(i, per) * tile + PAD, PAD)
            zq[comp, pl.ds(start, tile), :] = value
            zbq[rows, :] = value.astype(BF16)

    lower, upper = pl.ds(0, face), pl.ds(face, face)

    def faces_begin(field, out, into):
        tile = tile_of(face, 288, 16)
        waits = []
        for start in range(0, face, tile):
            for first, other, device in ((face, 0, above), (0, face, below)):
                rows, there = pl.ds(first + start, tile), pl.ds(other + start, tile)
                out[rows, :] = dot(pick[rows, :], field[...]).astype(BF16)
                waits.append(
                    remote(out.at[rows, :], into.at[there, :], device, into.at[there, :])
                )
        return waits

    def stencil(load, shift_of, store):
        size = tile_of(cells, 32, 16)

        @pl.loop(0, cells // size)
        def _(i):
            m0 = pl.multiple_of(i * size, size)
            blocks = [load(comp, pl.ds(m0, size + 2 * PAD)) for comp in range(3)]
            mid = [block[PAD : PAD + size] for block in blocks]
            total = 0.5 * (mid[0] + mid[1] + mid[2])
            for comp in range(3):
                rows = pl.ds(pl.multiple_of(comp * cells + m0, size), size)
                value = (6.5 + shift_of(rows)) * mid[comp] - total
                value -= blocks[comp][PAD - 1 : PAD - 1 + size]
                value -= blocks[comp][PAD + 1 : PAD + 1 + size]
                store(rows, value)

    def stencil_half(h):
        def store(rows, value):
            ubuf[h, rows, :] = value
            ub16[rows, :] = value.astype(BF16)

        stencil(lambda c, r: zpad[h, c, r, :], lambda r: twice(shift_col[r, :]), store)

    def stencil_quarter():
        def store(rows, value):
            yq[rows, :] = value

        stencil(lambda c, r: zq[c, r, :], lambda r: shift_col[r, :], store)

    def prepare(h):
        coarse = coarse_half(1, h)
        tile = tile_of(n, 768, 16)

        @pl.loop(0, n // tile)
        def _(i):
            rows = pl.ds(pl.multiple_of(i * tile, tile), tile)
            ubuf[h, rows, :] = local[1, h, rows, :].astype(F32) + dot(basis_t[rows, :], coarse)

    def fold(value):
        return jnp.sum(value.reshape(value.shape[0] // 8, 8, LANES), axis=0)

    def inner_products(terms):
        tile = tile_of(n, 768, 16)

        def step(i, sums):
            rows = pl.ds(pl.multiple_of(i * tile, tile), tile)
            return tuple(s + fold(t) for s, t in zip(sums, terms(rows)))

        zero = jnp.zeros((8, LANES), F32)
        sums = lax.fori_loop(0, n // tile, step, (zero, zero, zero))
        rows = [jnp.sum(value, axis=0, keepdims=True) for value in sums]
        return jnp.concatenate(rows + [jnp.zeros((5, LANES), F32)], axis=0)

    def first_terms(rows):
        b = side(bv[my_half, rows, :]).astype(F32)
        u = side(ubuf[my_half, rows, :] - 4.0 * dot(place[rows, :], frecv[my_half]))
        uq[rows, :] = u
        return b * b, u * b, u * u

    def second_terms(h11, rows):
        b = side(bv[my_half, rows, :]).astype(F32)
        u = uq[rows, :]
        g = yq[rows, :] - 4.0 * dot(place[rows, :], frecv_q[...]) - h11 * u
        t = u - h11 * b
        return g * b, g * t, g * g

    def reduce_begin(it, partial):
        rb1[it, j] = partial
        mine = rb1.at[it, j]
        return [
            remote(mine, mine, at_j(k), rb1.at[it, lax.rem(j + nj - k, nj)]) for k in range(1, nj)
        ]

    def reduce_z(it, waits):
        wait_all(waits)
        rb2[it, z] = jnp.sum(rb1[it], axis=0)
        mine = rb2.at[it, z]
        return [
            remote(mine, mine, at_z(k), rb2.at[it, lax.rem(z + nz - k, nz)]) for k in range(1, nz)
        ]

    def reduce_end(it, waits):
        wait_all(waits)
        total = jnp.sum(rb2[it], axis=0)
        return total[0:1], total[1:2], total[2:3]

    def build_pads():
        for i in range(n // LANES):
            block = wide[:, i * LANES : (i + 1) * LANES]
            basis_t[pl.ds(i * LANES, LANES), :] = block.T.astype(BF16)
        for h in range(2):
            for comp in range(3):
                for start in (0, cells + PAD):
                    zpad[h, comp, pl.ds(start, PAD), :] = jnp.zeros((PAD, HALF), F32)
        for comp in range(3):
            for start in (0, cells + PAD):
                zq[comp, pl.ds(start, PAD), :] = jnp.zeros((PAD, LANES), F32)
        for i in range(n // LANES):
            row = jnp.broadcast_to(shift_ref[:, i * LANES : (i + 1) * LANES], (LANES, LANES))
            shift_col[pl.ds(i * LANES, LANES), :] = row.T

    lane = lax.broadcasted_iota(jnp.int32, (LANES, LANES), 1)
    line = lax.broadcasted_iota(jnp.int32, (LANES, LANES), 0)

    face_all = jnp.concatenate([face_ref[0:1, :], face_ref[1:2, :]], axis=1)

    def face_row(i):
        return jnp.broadcast_to(face_all[:, i * LANES : (i + 1) * LANES], (LANES, LANES))

    def build_pick():
        for i in range(faces // LANES):
            column = face_row(i).astype(F32).T.astype(jnp.int32)
            for k in range(n // LANES):
                hit = jnp.where(column == lane + k * LANES, 1.0, 0.0)
                pick[pl.ds(i * LANES, LANES), k * LANES : (k + 1) * LANES] = hit.astype(BF16)

    def build_place():
        for i in range(faces // LANES):
            slot = lane + i * LANES
            missing = ((slot < face) & (me_s == 0)) | ((slot >= face) & (me_s == subs - 1))
            row = jnp.where(missing, -1, face_row(i))
            for k in range(n // LANES):
                hit = jnp.where(row == line + k * LANES, 1.0, 0.0)
                place[pl.ds(k * LANES, LANES), i * LANES : (i + 1) * LANES] = hit.astype(BF16)

    def build_inv_place():
        for start, size in tiles:
            rows = pl.ds(start, size)
            width = tile_of(faces, 384, LANES)

            @pl.loop(0, faces // width)
            def _(i):
                cols = pl.ds(pl.multiple_of(i * width, width), width)
                inv_place[rows, cols] = dot(inv[rows, :], place[:, cols]).astype(BF16)

    def ready(i):
        if i == 0:
            loads[0].wait()
        loads[1 + i].wait()

    part_begin()
    first_product(0, ready)
    g00 = gather_begin(0, 0, True)
    loads[3].wait()
    first_product(1)
    coarse = coarse_begin(0)
    build_pads()
    g00_near = gather_begin(0, 0, False)
    build_pick()
    g00 = gather_forward(0, 0, g00)
    build_place()
    part_end()
    coarse = coarse_line(0, coarse)
    build_inv_place()
    wait_all(g00_near)
    g01 = gather_begin(0, 1, True)
    coarse = coarse_end(0, coarse)
    wait_all(g00)
    wait_all(coarse)
    assemble(0)
    g01_near = gather_begin(0, 1, False)
    f00 = faces_begin(zb, fsend.at[0], frecv.at[0])
    stencil_half(0)
    g01 = gather_forward(0, 1, g01)

    second_product(0)
    second_faces(0, f00)
    g10 = gather_begin(1, 0, True)
    wait_all(g01_near)
    wait_all(g01)
    assemble(1)
    f01 = faces_begin(zb, fsend.at[1], frecv.at[1])
    g10_near = gather_begin(1, 0, False)
    stencil_half(1)
    second_product(1)
    g10 = gather_forward(1, 0, g10)
    second_faces(1, f01)
    coarse = coarse_begin(1)

    prio_sem = used[0]
    used[0] += ny - 1
    own_part = pl.ds(base, nq)

    def prio_copy(k):
        target = lax.rem(me_y + k, ny)
        col = pl.multiple_of(lax.rem(target, 2) * LANES, LANES)
        return target, describe(
            prio_sem + k - 1,
            local.at[1, 1, own_part, pl.ds(col, LANES)],
            prio.at[own_part, :],
            at_y(k),
        )

    def prio_begin():
        for k in range(1, ny):
            target, cp = prio_copy(k)

            @pl.when(target // 2 == 1)
            def _(cp=cp):
                cp.start()

        @pl.when(my_half == 1)
        def _():
            prio[own_part, :] = side(local[1, 1, own_part, :].astype(F32)).astype(BF16)

    def prio_end():
        for k in range(1, ny):
            target, cp = prio_copy(k)

            @pl.when(target // 2 == 1)
            def _(cp=cp):
                cp.wait_send()

        @pl.when(my_half == 1)
        def _():
            for k in range(1, ny):
                source = lax.rem(me_y + ny - k, ny)
                slot = prio.at[pl.ds(pl.multiple_of(source * nq, nq), nq), :]
                describe(prio_sem + k - 1, slot, slot, at_y(k)).wait_recv()

    prio_begin()
    r0 = reduce_begin(0, inner_products(first_terms))
    coarse = coarse_line(1, coarse)
    g11 = gather_begin(1, 1, True)
    r0 = reduce_z(0, r0)
    g11_near = gather_begin(1, 1, False)
    coarse = coarse_end(1, coarse)
    prio_end()
    wait_all(g10_near)
    wait_all(g10)

    @pl.when(my_half == 0)
    def _():
        assemble_quarter(lambda rows: side(local[1, 0, rows, :].astype(F32)))

    @pl.when(my_half == 1)
    def _():
        assemble_quarter(lambda rows: prio[rows, :])

    f1 = faces_begin(zbq, fsend_q, frecv_q)
    g11 = gather_forward(1, 1, g11)
    bb, ub, uu = reduce_end(0, r0)
    stencil_quarter()
    beta2 = bb + 1e-12
    beta = jnp.sqrt(beta2)
    h11 = ub / beta2
    h21s = jnp.maximum((uu - h11 * (2.0 * ub - h11 * bb)) / beta2, 0.0) + 1e-12
    h21 = jnp.sqrt(h21s)
    wait_all(f1)
    r1 = reduce_begin(1, inner_products(functools.partial(second_terms, h11)))
    wait_all(coarse)
    prepare(0)
    r1 = reduce_z(1, r1)
    wait_all(g11_near)
    wait_all(g11)
    prepare(1)
    gb, gt, gg = reduce_end(1, r1)

    scale = 1.0 / (beta * h21)
    h12 = gb * scale / beta
    h22 = gt * scale * scale
    ww = gg * scale * scale
    ff_gap = 1e-12 / beta2
    ss_gap = 1e-12 / h21s
    fs = h11 * ff_gap / h21
    h32s = ww - h12 * h12 * (1.0 + ff_gap) - h22 * h22 * (1.0 + ss_gap) + 2.0 * h12 * h22 * fs
    h32 = jnp.sqrt(jnp.maximum(h32s, 0.0) + 1e-12)
    dist_one = jnp.sqrt(h11 * h11 + h21 * h21)
    cos_one = h11 / dist_one
    sin_one = h21 / dist_one
    r12 = cos_one * h12 + sin_one * h22
    t22 = cos_one * h22 - sin_one * h12
    dist_two = jnp.sqrt(t22 * t22 + h32 * h32)
    cos_two = t22 / dist_two
    sin_two = h32 / dist_two
    y2 = -cos_two * sin_one * beta / dist_two
    y1 = (cos_one * beta - r12 * y2) / dist_one
    weight_two = y2 * scale
    weight_one = y1 / beta - h11 * weight_two
    residual = jnp.abs(sin_one * sin_two)
    weights[me_y] = jnp.concatenate(
        [weight_one, weight_two, residual, jnp.zeros((5, LANES), F32)], axis=0
    )
    mine = weights.at[me_y]
    w1 = [
        remote(mine, mine, at_y(k), weights.at[lax.rem(me_y + ny - k, ny)]) for k in range(1, ny)
    ]

    def finish(h):
        def pair(i):
            return jnp.concatenate([weights[2 * h, i : i + 1], weights[2 * h + 1, i : i + 1]], axis=1)

        one_w, two_w, res = pair(0), pair(1), pair(2)
        res_ref[:, h * HALF : (h + 1) * HALF] = res
        tile = tile_of(cells, 256, 16)
        outs = []
        for comp in range(3):

            @pl.loop(0, cells // tile)
            def _(i, comp=comp):
                m0 = pl.multiple_of(i * tile, tile)
                rows = pl.ds(pl.multiple_of(comp * cells + m0, tile), tile)
                one = zpad[h, comp, pl.ds(m0 + PAD, tile), :]
                bv[h, rows, :] = (one * one_w + ubuf[h, rows, :] * two_w).astype(BF16)

            rows = pl.ds(comp * cells, cells)
            out = pltpu.make_async_copy(
                bv.at[h, rows, :],
                sol_hbm.at[rows, pl.ds(h * HALF, HALF)],
                lsem.at[5 + 3 * h + comp],
            )
            out.start()
            outs.append(out)
        return outs

    wait_all(w1)
    outs = finish(0)
    outs += finish(1)
    for cp in sent:
        cp.wait_send()
    for cp in outs:
        cp.wait()
    assert used[0] <= ssem.shape[0]


def count_copies(nz, nx, ny, rims):
    line, group = nz - 1, 2 * nx - 1
    coarse = 2 * (line + group + ny - 1)
    return 3 * (ny - 1) + coarse + 4 * 6 + 3 * rims + 2 * (group + line)


def per_device(nz, nx, right_sides, shift, inverses, basis, counts, face_rows, coarse_inverse):
    ny = lax.axis_size("crs")
    n, width = right_sides.shape[1:]
    nq = n // ny
    kmax = basis.shape[1]
    faces = 2 * face_rows.shape[2]
    cells = n // 3
    nj = 2 * nx
    subs = nz * nj
    ext = nq + kmax
    copies = count_copies(nz, nx, ny, 2 * (faces // 2 // tile_of(faces // 2, 288, 16)))
    any_spec = pl.BlockSpec(memory_space=pl.ANY)
    vmem = pl.BlockSpec(memory_space=pltpu.VMEM)
    out, residual = pl.pallas_call(
        functools.partial(kernel, (nz, nx, ny)),
        out_shape=(
            jax.ShapeDtypeStruct((n, width), BF16),
            jax.ShapeDtypeStruct((1, width), F32),
        ),
        in_specs=[
            any_spec,
            any_spec,
            any_spec,
            vmem,
            vmem,
            pl.BlockSpec(memory_space=pltpu.SMEM),
            vmem,
        ],
        out_specs=(any_spec, vmem),
        scratch_shapes=[
            pltpu.VMEM((2, n, HALF), BF16),
            pltpu.VMEM((ext, n), BF16),
            pltpu.VMEM((n, LANES), BF16),
            pltpu.VMEM((LANES, n), F32),
            pltpu.VMEM((n, LANES), F32),
            pltpu.VMEM((faces, n), BF16),
            pltpu.VMEM((n, faces), BF16),
            pltpu.VMEM((ext, faces), BF16),
            pltpu.VMEM((ext, HALF), F32),
            pltpu.VMEM((2, 2, n, HALF), BF16),
            pltpu.VMEM((n, LANES), BF16),
            pltpu.VMEM((2, 3, cells + 2 * PAD, HALF), F32),
            pltpu.VMEM((n, HALF), BF16),
            pltpu.VMEM((2, n, HALF), F32),
            pltpu.VMEM((n, HALF), BF16),
            pltpu.VMEM((2, faces, HALF), BF16),
            pltpu.VMEM((2, faces, HALF), BF16),
            pltpu.VMEM((3, cells + 2 * PAD, LANES), F32),
            pltpu.VMEM((n, LANES), BF16),
            pltpu.VMEM((n, LANES), F32),
            pltpu.VMEM((n, LANES), F32),
            pltpu.VMEM((faces, LANES), BF16),
            pltpu.VMEM((faces, LANES), BF16),
            pltpu.VMEM((nj * kmax, subs * kmax), BF16),
            pltpu.VMEM((subs * kmax, nz * kmax), BF16),
            pltpu.VMEM((nj * kmax, nz * kmax), BF16),
            pltpu.VMEM((2, 2, kmax, HALF), F32),
            pltpu.VMEM((2, nz, kmax, LANES), BF16),
            pltpu.VMEM((2, nj, kmax, LANES), F32),
            pltpu.VMEM((2, nj, kmax, LANES), F32),
            pltpu.VMEM((2, ny, kmax, LANES), BF16),
            pltpu.VMEM((2, nj, 8, LANES), F32),
            pltpu.VMEM((2, nz, 8, LANES), F32),
            pltpu.VMEM((ny, 8, LANES), F32),
            pltpu.SemaphoreType.DMA((copies,)),
            pltpu.SemaphoreType.DMA((copies,)),
            pltpu.SemaphoreType.DMA((11,)),
        ],
        compiler_params=pltpu.CompilerParams(
            collective_id=0, has_side_effects=True, vmem_limit_bytes=60 * 1024 * 1024
        ),
    )(
        right_sides[0],
        inverses[0],
        coarse_inverse,
        shift,
        basis[0],
        counts,
        face_rows[0],
    )
    return out[None], residual.reshape(width)


def solution(mesh):
    subs = mesh.shape["sub"]
    nz = 8 if subs == 64 else subs // 2
    nx = subs // (2 * nz)
    return jax.shard_map(
        functools.partial(per_device, nz, nx),
        mesh=mesh,
        in_specs=(
            P("sub", None, None),
            P("sub", None),
            P("sub", "crs", None),
            P("sub", None, None),
            P("sub"),
            P("sub", None, None),
            P("crs", None),
        ),
        out_specs=(P("sub", None, None), P()),
        check_vma=False,
    )
```

```python
import functools

import jax
import jax.numpy as jnp
from jax import lax
from jax.experimental import pallas as pl
from jax.experimental.pallas import tpu as pltpu
from jax.sharding import PartitionSpec as P

MESH = pl.DeviceIdType.MESH
F32 = jnp.float32
BF16 = jnp.bfloat16
LANES = 128
HALF = 256
PAD = 8


def dot(a, b):
    return jnp.dot(a, b, preferred_element_type=F32)


def twice(block):
    return jnp.concatenate([block, block], axis=1)


def tile_of(rows, most, unit):
    tile = unit
    for size in range(unit, most + 1, unit):
        if rows % size == 0:
            tile = size
    return tile


def kernel(
    plan,
    b_hbm,
    inv_hbm,
    cinv_hbm,
    shift_ref,
    basis_ref,
    count_ref,
    face_ref,
    sol_hbm,
    res_ref,
    bv,
    inv,
    basis_t,
    wide,
    shift_col,
    pick,
    place,
    inv_place,
    acc,
    local,
    prio,
    zpad,
    zb,
    ubuf,
    ub16,
    fsend,
    frecv,
    zq,
    zbq,
    yq,
    uq,
    fsend_q,
    frecv_q,
    cpart,
    coef,
    cg,
    cpsend,
    cprecv,
    co,
    rb1,
    rb2,
    weights,
    ssem,
    rsem,
    lsem,
):
    nz, nx, ny = plan
    nj = 2 * nx
    subs = nz * nj
    kmax, n = basis_ref.shape
    cells = n // 3
    nq = n // ny
    hq = nq // 2
    face = face_ref.shape[1]
    faces = 2 * face

    me_s = lax.axis_index("sub")
    me_y = lax.axis_index("crs")
    j = lax.rem(me_s, nj)
    z = me_s // nj
    my_half = me_y // 2
    my_side = lax.rem(me_y, 2)

    def at_y(k):
        return (me_s, lax.rem(me_y + k, ny))

    def at_z(k):
        return (lax.rem(z + k, nz) * nj + j, me_y)

    def at_j(k):
        return (z * nj + lax.rem(j + k, nj), me_y)

    above = (lax.rem(me_s + 1, subs), me_y)
    below = (lax.rem(me_s + subs - 1, subs), me_y)

    def side(block):
        return jnp.where(my_side == 0, block[:, :LANES], block[:, LANES:])

    used = [0]
    sent = []

    def describe(i, src, dst, device):
        return pltpu.make_async_remote_copy(
            src_ref=src,
            dst_ref=dst,
            send_sem=ssem.at[i],
            recv_sem=rsem.at[i],
            device_id=device,
            device_id_type=MESH,
        )

    def remote(src, dst, device, slot):
        i = used[0]
        used[0] += 1
        cp = describe(i, src, dst, device)
        cp.start()
        sent.append(cp)
        arrived = describe(i, slot, slot, device)
        return arrived

    def wait_all(waits):
        for w in waits:
            w.wait_recv()

    ext = nq + kmax
    cut = ext // 2
    tiles = ((0, cut), (cut, ext - cut))

    def load_b(h):
        return pltpu.make_async_copy(b_hbm.at[:, pl.ds(h * HALF, HALF)], bv.at[h], lsem.at[h])

    def load_inv(i):
        rows = pl.ds(tiles[i][0], min(tiles[i][1], nq - tiles[i][0]))
        return pltpu.make_async_copy(inv_hbm.at[rows, :], inv.at[rows, :], lsem.at[2 + i])

    loads = [load_b(0), load_inv(0), load_inv(1), load_b(1)]
    for cp in loads:
        cp.start()

    barrier = pltpu.get_barrier_semaphore()
    partners = [at_y(k) for k in range(1, ny)] + [at_z(k) for k in range(1, nz)]
    partners += [at_j(k) for k in range(1, nj)] + [above, below]
    for device in partners:
        pl.semaphore_signal(barrier, inc=1, device_id=device, device_id_type=MESH)

    keep = lax.broadcasted_iota(jnp.int32, (kmax, n), 0) < count_ref[0]
    masked = jnp.where(keep, basis_ref[...].astype(F32), 0.0)
    inv[pl.ds(nq, kmax), :] = masked.astype(BF16)
    wide[...] = jnp.zeros_like(wide)
    wide[pl.ds(0, kmax), :] = masked

    pl.semaphore_wait(barrier, len(partners))

    mine_z = cinv_hbm.shape[0]
    part_sem = used[0]
    used[0] += ny - 1
    wanted = cinv_hbm.at[:, j, :, pl.ds(pl.multiple_of(z * nj * kmax, nj * kmax), nj * kmax)]

    def part_slot(k):
        return cpart.at[pl.ds(lax.rem(me_y + k, ny) * mine_z, mine_z)]

    own_part_copy = pltpu.make_async_copy(wanted, part_slot(0), lsem.at[4])
    own_part_copy.start()

    def part_begin():
        for k in range(1, ny):
            describe(part_sem + k - 1, wanted, part_slot(0), at_y(k)).start()

    def part_end():
        own_part_copy.wait()
        for k in range(1, ny):
            describe(part_sem + k - 1, wanted, part_slot(0), at_y(k)).wait_send()
            slot = part_slot(ny - k)
            describe(part_sem + k - 1, slot, slot, at_y(k)).wait_recv()

    def coarse_begin(it):
        cg[it, j] = side(coef[it, my_half]).astype(BF16)
        mine = cg.at[it, j]
        return [
            remote(mine, mine, at_j(k), cg.at[it, lax.rem(j + nj - k, nj)]) for k in range(1, nj)
        ]

    def coarse_line(it, waits):
        wait_all(waits)
        rows = cpart[...].reshape(nz * kmax, nj * kmax)
        partial = dot(rows, cg[it].reshape(nj * kmax, LANES))
        cpsend[it] = partial.reshape(nz, kmax, LANES)
        cprecv[it, z] = cpsend[it, z]
        return [
            remote(
                cpsend.at[it, lax.rem(z + k, nz)],
                cprecv.at[it, z],
                at_z(k),
                cprecv.at[it, lax.rem(z + nz - k, nz)],
            )
            for k in range(1, nz)
        ]

    def coarse_end(it, waits):
        wait_all(waits)
        co[it, me_y] = jnp.sum(cprecv[it], axis=0).astype(BF16)
        mine = co.at[it, me_y]
        return [
            remote(mine, mine, at_y(k), co.at[it, lax.rem(me_y + ny - k, ny)])
            for k in range(1, ny)
        ]

    base = pl.multiple_of(me_y * nq, nq)
    right, left = at_y(1), at_y(ny - 1)

    def part_rows(k, low):
        owner_y = lax.rem(me_y + k, ny)
        return pl.ds(pl.multiple_of(owner_y * nq + (0 if low else hq), hq), hq)

    def keep_product(it, h, start, size, out):
        rows = min(size, nq - start)
        local[it, h, pl.ds(pl.multiple_of(base + start, 16), rows), :] = out[:rows].astype(BF16)
        if rows < size:
            coef[it, h] = out[rows:]

    def first_product(h, ready=None):
        for i, (start, size) in enumerate(tiles):
            if ready is not None:
                ready(i)
            keep_product(0, h, start, size, dot(inv[pl.ds(start, size), :], bv[h]))

    def second_product(h):
        for start, size in tiles:
            acc[pl.ds(start, size), :] = dot(inv[pl.ds(start, size), :], ub16[...])

    def second_faces(h, waits):
        wait_all(waits)
        for start, size in tiles:
            rows = pl.ds(start, size)
            out = acc[rows, :] - 4.0 * dot(inv_place[rows, :], frecv[h])
            keep_product(1, h, start, size, out)

    def gather_begin(it, h, first):
        buf = local.at[it, h]

        def send(k, low, device):
            mine = buf.at[part_rows(0, low), :]
            return remote(mine, mine, device, buf.at[part_rows(k, low), :])

        if first:
            return send(ny - 1, True, right), send(1, False, left)
        return send(ny - 1, False, right), send(1, True, left)

    def gather_forward(it, h, waits):
        buf = local.at[it, h]
        waits[0].wait_recv()
        low = buf.at[part_rows(ny - 1, True), :]
        far_low = remote(low, low, right, buf.at[part_rows(2, True), :])
        waits[1].wait_recv()
        high = buf.at[part_rows(1, False), :]
        far_high = remote(high, high, left, buf.at[part_rows(2, False), :])
        return far_low, far_high

    def padded(block):
        rest = jnp.zeros((LANES - kmax, block.shape[1]), BF16)
        return jnp.concatenate([block, rest], axis=0)

    def coarse_half(it, h):
        return padded(jnp.concatenate([co[it, 2 * h], co[it, 2 * h + 1]], axis=1))

    def assemble(h):
        coarse = coarse_half(0, h)
        tile = tile_of(cells, 768, 16)
        per = cells // tile

        @pl.loop(0, 3 * per)
        def _(i):
            comp = i // per
            rows = pl.ds(pl.multiple_of(i * tile, tile), tile)
            value = local[0, h, rows, :].astype(F32) + dot(basis_t[rows, :], coarse)
            start = pl.multiple_of(lax.rem(i, per) * tile + PAD, PAD)
            zpad[h, comp, pl.ds(start, tile), :] = value
            zb[rows, :] = value.astype(BF16)

    def assemble_quarter(field):
        coarse = padded(co[1, me_y])
        tile = tile_of(cells, 768, 16)
        per = cells // tile

        @pl.loop(0, 3 * per)
        def _(i):
            comp = i // per
            rows = pl.ds(pl.multiple_of(i * tile, tile), tile)
            value = field(rows).astype(F32) + dot(basis_t[rows, :], coarse)
            start = pl.multiple_of(lax.rem(i, per) * tile + PAD, PAD)
            zq[comp, pl.ds(start, tile), :] = value
            zbq[rows, :] = value.astype(BF16)

    lower, upper = pl.ds(0, face), pl.ds(face, face)

    def faces_begin(field, out, into):
        tile = tile_of(face, 288, 16)
        waits = []
        for start in range(0, face, tile):
            for first, other, device in ((face, 0, above), (0, face, below)):
                rows, there = pl.ds(first + start, tile), pl.ds(other + start, tile)
                out[rows, :] = dot(pick[rows, :], field[...]).astype(BF16)
                waits.append(
                    remote(out.at[rows, :], into.at[there, :], device, into.at[there, :])
                )
        return waits

    def stencil(load, shift_of, store):
        size = tile_of(cells, 32, 16)

        @pl.loop(0, cells // size)
        def _(i):
            m0 = pl.multiple_of(i * size, size)
            blocks = [load(comp, pl.ds(m0, size + 2 * PAD)) for comp in range(3)]
            mid = [block[PAD : PAD + size] for block in blocks]
            total = 0.5 * (mid[0] + mid[1] + mid[2])
            for comp in range(3):
                rows = pl.ds(pl.multiple_of(comp * cells + m0, size), size)
                value = (6.5 + shift_of(rows)) * mid[comp] - total
                value -= blocks[comp][PAD - 1 : PAD - 1 + size]
                value -= blocks[comp][PAD + 1 : PAD + 1 + size]
                store(rows, value)

    def stencil_half(h):
        def store(rows, value):
            ubuf[h, rows, :] = value
            ub16[rows, :] = value.astype(BF16)

        stencil(lambda c, r: zpad[h, c, r, :], lambda r: twice(shift_col[r, :]), store)

    def stencil_quarter():
        def store(rows, value):
            yq[rows, :] = value

        stencil(lambda c, r: zq[c, r, :], lambda r: shift_col[r, :], store)

    def prepare(h):
        coarse = coarse_half(1, h)
        tile = tile_of(n, 768, 16)

        @pl.loop(0, n // tile)
        def _(i):
            rows = pl.ds(pl.multiple_of(i * tile, tile), tile)
            ubuf[h, rows, :] = local[1, h, rows, :].astype(F32) + dot(basis_t[rows, :], coarse)

    def fold(value):
        return jnp.sum(value.reshape(value.shape[0] // 8, 8, LANES), axis=0)

    def inner_products(terms):
        tile = tile_of(n, 768, 16)

        def step(i, sums):
            rows = pl.ds(pl.multiple_of(i * tile, tile), tile)
            return tuple(s + fold(t) for s, t in zip(sums, terms(rows)))

        zero = jnp.zeros((8, LANES), F32)
        sums = lax.fori_loop(0, n // tile, step, (zero, zero, zero))
        rows = [jnp.sum(value, axis=0, keepdims=True) for value in sums]
        return jnp.concatenate(rows + [jnp.zeros((5, LANES), F32)], axis=0)

    def first_terms(rows):
        b = side(bv[my_half, rows, :]).astype(F32)
        u = side(ubuf[my_half, rows, :] - 4.0 * dot(place[rows, :], frecv[my_half]))
        uq[rows, :] = u
        return b * b, u * b, u * u

    def second_terms(h11, rows):
        b = side(bv[my_half, rows, :]).astype(F32)
        u = uq[rows, :]
        g = yq[rows, :] - 4.0 * dot(place[rows, :], frecv_q[...]) - h11 * u
        t = u - h11 * b
        return g * b, g * t, g * g

    def reduce_begin(it, partial):
        rb1[it, j] = partial
        mine = rb1.at[it, j]
        return [
            remote(mine, mine, at_j(k), rb1.at[it, lax.rem(j + nj - k, nj)]) for k in range(1, nj)
        ]

    def reduce_z(it, waits):
        wait_all(waits)
        rb2[it, z] = jnp.sum(rb1[it], axis=0)
        mine = rb2.at[it, z]
        return [
            remote(mine, mine, at_z(k), rb2.at[it, lax.rem(z + nz - k, nz)]) for k in range(1, nz)
        ]

    def reduce_end(it, waits):
        wait_all(waits)
        total = jnp.sum(rb2[it], axis=0)
        return total[0:1], total[1:2], total[2:3]

    def build_pads():
        for i in range(n // LANES):
            block = wide[:, i * LANES : (i + 1) * LANES]
            basis_t[pl.ds(i * LANES, LANES), :] = block.T.astype(BF16)
        for h in range(2):
            for comp in range(3):
                for start in (0, cells + PAD):
                    zpad[h, comp, pl.ds(start, PAD), :] = jnp.zeros((PAD, HALF), F32)
        for comp in range(3):
            for start in (0, cells + PAD):
                zq[comp, pl.ds(start, PAD), :] = jnp.zeros((PAD, LANES), F32)
        for i in range(n // LANES):
            row = jnp.broadcast_to(shift_ref[:, i * LANES : (i + 1) * LANES], (LANES, LANES))
            shift_col[pl.ds(i * LANES, LANES), :] = row.T

    lane = lax.broadcasted_iota(jnp.int32, (LANES, LANES), 1)
    line = lax.broadcasted_iota(jnp.int32, (LANES, LANES), 0)

    face_all = jnp.concatenate([face_ref[0:1, :], face_ref[1:2, :]], axis=1)

    def face_row(i):
        return jnp.broadcast_to(face_all[:, i * LANES : (i + 1) * LANES], (LANES, LANES))

    def build_pick():
        for i in range(faces // LANES):
            column = face_row(i).astype(F32).T.astype(jnp.int32)
            for k in range(n // LANES):
                hit = jnp.where(column == lane + k * LANES, 1.0, 0.0)
                pick[pl.ds(i * LANES, LANES), k * LANES : (k + 1) * LANES] = hit.astype(BF16)

    def build_place():
        for i in range(faces // LANES):
            slot = lane + i * LANES
            missing = ((slot < face) & (me_s == 0)) | ((slot >= face) & (me_s == subs - 1))
            row = jnp.where(missing, -1, face_row(i))
            for k in range(n // LANES):
                hit = jnp.where(row == line + k * LANES, 1.0, 0.0)
                place[pl.ds(k * LANES, LANES), i * LANES : (i + 1) * LANES] = hit.astype(BF16)

    def build_inv_place():
        for start, size in tiles:
            rows = pl.ds(start, size)
            width = tile_of(faces, 384, LANES)

            @pl.loop(0, faces // width)
            def _(i):
                cols = pl.ds(pl.multiple_of(i * width, width), width)
                inv_place[rows, cols] = dot(inv[rows, :], place[:, cols]).astype(BF16)

    def ready(i):
        if i == 0:
            loads[0].wait()
        loads[1 + i].wait()

    part_begin()
    first_product(0, ready)
    g00 = gather_begin(0, 0, True)
    loads[3].wait()
    first_product(1)
    coarse = coarse_begin(0)
    build_pads()
    g00_near = gather_begin(0, 0, False)
    build_pick()
    g00 = gather_forward(0, 0, g00)
    build_place()
    part_end()
    coarse = coarse_line(0, coarse)
    build_inv_place()
    wait_all(g00_near)
    g01 = gather_begin(0, 1, True)
    coarse = coarse_end(0, coarse)
    wait_all(g00)
    wait_all(coarse)
    assemble(0)
    g01_near = gather_begin(0, 1, False)
    f00 = faces_begin(zb, fsend.at[0], frecv.at[0])
    stencil_half(0)
    g01 = gather_forward(0, 1, g01)

    second_product(0)
    second_faces(0, f00)
    g10 = gather_begin(1, 0, True)
    wait_all(g01_near)
    wait_all(g01)
    assemble(1)
    f01 = faces_begin(zb, fsend.at[1], frecv.at[1])
    g10_near = gather_begin(1, 0, False)
    stencil_half(1)
    second_product(1)
    g10 = gather_forward(1, 0, g10)
    second_faces(1, f01)
    coarse = coarse_begin(1)

    prio_sem = used[0]
    used[0] += ny - 1
    own_part = pl.ds(base, nq)

    def prio_copy(k):
        target = lax.rem(me_y + k, ny)
        col = pl.multiple_of(lax.rem(target, 2) * LANES, LANES)
        return target, describe(
            prio_sem + k - 1,
            local.at[1, 1, own_part, pl.ds(col, LANES)],
            prio.at[own_part, :],
            at_y(k),
        )

    def prio_begin():
        for k in range(1, ny):
            target, cp = prio_copy(k)

            @pl.when(target // 2 == 1)
            def _(cp=cp):
                cp.start()

        @pl.when(my_half == 1)
        def _():
            prio[own_part, :] = side(local[1, 1, own_part, :].astype(F32)).astype(BF16)

    def prio_end():
        for k in range(1, ny):
            target, cp = prio_copy(k)

            @pl.when(target // 2 == 1)
            def _(cp=cp):
                cp.wait_send()

        @pl.when(my_half == 1)
        def _():
            for k in range(1, ny):
                source = lax.rem(me_y + ny - k, ny)
                slot = prio.at[pl.ds(pl.multiple_of(source * nq, nq), nq), :]
                describe(prio_sem + k - 1, slot, slot, at_y(k)).wait_recv()

    prio_begin()
    r0 = reduce_begin(0, inner_products(first_terms))
    coarse = coarse_line(1, coarse)
    g11 = gather_begin(1, 1, True)
    r0 = reduce_z(0, r0)
    g11_near = gather_begin(1, 1, False)
    coarse = coarse_end(1, coarse)
    prio_end()
    wait_all(g10_near)
    wait_all(g10)

    @pl.when(my_half == 0)
    def _():
        assemble_quarter(lambda rows: side(local[1, 0, rows, :].astype(F32)))

    @pl.when(my_half == 1)
    def _():
        assemble_quarter(lambda rows: prio[rows, :])

    f1 = faces_begin(zbq, fsend_q, frecv_q)
    g11 = gather_forward(1, 1, g11)
    bb, ub, uu = reduce_end(0, r0)
    stencil_quarter()
    beta2 = bb + 1e-12
    beta = jnp.sqrt(beta2)
    h11 = ub / beta2
    h21s = jnp.maximum((uu - h11 * (2.0 * ub - h11 * bb)) / beta2, 0.0) + 1e-12
    h21 = jnp.sqrt(h21s)
    wait_all(f1)
    r1 = reduce_begin(1, inner_products(functools.partial(second_terms, h11)))
    wait_all(coarse)
    prepare(0)
    r1 = reduce_z(1, r1)
    wait_all(g11_near)
    wait_all(g11)
    prepare(1)
    gb, gt, gg = reduce_end(1, r1)

    scale = 1.0 / (beta * h21)
    h12 = gb * scale / beta
    h22 = gt * scale * scale
    ww = gg * scale * scale
    ff_gap = 1e-12 / beta2
    ss_gap = 1e-12 / h21s
    fs = h11 * ff_gap / h21
    h32s = ww - h12 * h12 * (1.0 + ff_gap) - h22 * h22 * (1.0 + ss_gap) + 2.0 * h12 * h22 * fs
    h32 = jnp.sqrt(jnp.maximum(h32s, 0.0) + 1e-12)
    dist_one = jnp.sqrt(h11 * h11 + h21 * h21)
    cos_one = h11 / dist_one
    sin_one = h21 / dist_one
    r12 = cos_one * h12 + sin_one * h22
    t22 = cos_one * h22 - sin_one * h12
    dist_two = jnp.sqrt(t22 * t22 + h32 * h32)
    cos_two = t22 / dist_two
    sin_two = h32 / dist_two
    y2 = -cos_two * sin_one * beta / dist_two
    y1 = (cos_one * beta - r12 * y2) / dist_one
    weight_two = y2 * scale
    weight_one = y1 / beta - h11 * weight_two
    residual = jnp.abs(sin_one * sin_two)
    weights[me_y] = jnp.concatenate(
        [weight_one, weight_two, residual, jnp.zeros((5, LANES), F32)], axis=0
    )
    mine = weights.at[me_y]
    w1 = [
        remote(mine, mine, at_y(k), weights.at[lax.rem(me_y + ny - k, ny)]) for k in range(1, ny)
    ]

    def finish(h):
        def pair(i):
            return jnp.concatenate([weights[2 * h, i : i + 1], weights[2 * h + 1, i : i + 1]], axis=1)

        one_w, two_w, res = pair(0), pair(1), pair(2)
        res_ref[:, h * HALF : (h + 1) * HALF] = res
        tile = tile_of(cells, 256, 16)
        outs = []
        for comp in range(3):

            @pl.loop(0, cells // tile)
            def _(i, comp=comp):
                m0 = pl.multiple_of(i * tile, tile)
                rows = pl.ds(pl.multiple_of(comp * cells + m0, tile), tile)
                one = zpad[h, comp, pl.ds(m0 + PAD, tile), :]
                bv[h, rows, :] = (one * one_w + ubuf[h, rows, :] * two_w).astype(BF16)

            rows = pl.ds(comp * cells, cells)
            out = pltpu.make_async_copy(
                bv.at[h, rows, :],
                sol_hbm.at[rows, pl.ds(h * HALF, HALF)],
                lsem.at[5 + 3 * h + comp],
            )
            out.start()
            outs.append(out)
        return outs

    wait_all(w1)
    outs = finish(0)
    outs += finish(1)
    for cp in sent:
        cp.wait_send()
    for cp in outs:
        cp.wait()
    assert used[0] <= ssem.shape[0]


def count_copies(nz, nx, ny, rims):
    line, group = nz - 1, 2 * nx - 1
    coarse = 2 * (line + group + ny - 1)
    return 3 * (ny - 1) + coarse + 4 * 6 + 3 * rims + 2 * (group + line)


def per_device(nz, nx, right_sides, shift, inverses, basis, counts, face_rows, coarse_inverse):
    ny = lax.axis_size("crs")
    n, width = right_sides.shape[1:]
    nq = n // ny
    kmax = basis.shape[1]
    faces = 2 * face_rows.shape[2]
    cells = n // 3
    nj = 2 * nx
    subs = nz * nj
    ext = nq + kmax
    copies = count_copies(nz, nx, ny, 2 * (faces // 2 // tile_of(faces // 2, 288, 16)))
    any_spec = pl.BlockSpec(memory_space=pl.ANY)
    vmem = pl.BlockSpec(memory_space=pltpu.VMEM)
    out, residual = pl.pallas_call(
        functools.partial(kernel, (nz, nx, ny)),
        out_shape=(
            jax.ShapeDtypeStruct((n, width), BF16),
            jax.ShapeDtypeStruct((1, width), F32),
        ),
        in_specs=[
            any_spec,
            any_spec,
            any_spec,
            vmem,
            vmem,
            pl.BlockSpec(memory_space=pltpu.SMEM),
            vmem,
        ],
        out_specs=(any_spec, vmem),
        scratch_shapes=[
            pltpu.VMEM((2, n, HALF), BF16),
            pltpu.VMEM((ext, n), BF16),
            pltpu.VMEM((n, LANES), BF16),
            pltpu.VMEM((LANES, n), F32),
            pltpu.VMEM((n, LANES), F32),
            pltpu.VMEM((faces, n), BF16),
            pltpu.VMEM((n, faces), BF16),
            pltpu.VMEM((ext, faces), BF16),
            pltpu.VMEM((ext, HALF), F32),
            pltpu.VMEM((2, 2, n, HALF), BF16),
            pltpu.VMEM((n, LANES), BF16),
            pltpu.VMEM((2, 3, cells + 2 * PAD, HALF), F32),
            pltpu.VMEM((n, HALF), BF16),
            pltpu.VMEM((2, n, HALF), F32),
            pltpu.VMEM((n, HALF), BF16),
            pltpu.VMEM((2, faces, HALF), BF16),
            pltpu.VMEM((2, faces, HALF), BF16),
            pltpu.VMEM((3, cells + 2 * PAD, LANES), F32),
            pltpu.VMEM((n, LANES), BF16),
            pltpu.VMEM((n, LANES), F32),
            pltpu.VMEM((n, LANES), F32),
            pltpu.VMEM((faces, LANES), BF16),
            pltpu.VMEM((faces, LANES), BF16),
            pltpu.VMEM((nz, kmax, nj * kmax), BF16),
            pltpu.VMEM((2, 2, kmax, HALF), F32),
            pltpu.VMEM((2, nj, kmax, LANES), BF16),
            pltpu.VMEM((2, nz, kmax, LANES), F32),
            pltpu.VMEM((2, nz, kmax, LANES), F32),
            pltpu.VMEM((2, ny, kmax, LANES), BF16),
            pltpu.VMEM((2, nj, 8, LANES), F32),
            pltpu.VMEM((2, nz, 8, LANES), F32),
            pltpu.VMEM((ny, 8, LANES), F32),
            pltpu.SemaphoreType.DMA((copies,)),
            pltpu.SemaphoreType.DMA((copies,)),
            pltpu.SemaphoreType.DMA((11,)),
        ],
        compiler_params=pltpu.CompilerParams(
            collective_id=0, has_side_effects=True, vmem_limit_bytes=60 * 1024 * 1024
        ),
    )(
        right_sides[0],
        inverses[0],
        coarse_inverse.reshape(-1, nj, kmax, subs * kmax),
        shift,
        basis[0],
        counts,
        face_rows[0],
    )
    return out[None], residual.reshape(width)


def solution(mesh):
    subs = mesh.shape["sub"]
    nz = 8 if subs == 64 else subs // 2
    nx = subs // (2 * nz)
    return jax.shard_map(
        functools.partial(per_device, nz, nx),
        mesh=mesh,
        in_specs=(
            P("sub", None, None),
            P("sub", None),
            P("sub", "crs", None),
            P("sub", None, None),
            P("sub"),
            P("sub", None, None),
            P("crs", None),
        ),
        out_specs=(P("sub", None, None), P()),
        check_vma=False,
    )
```

```python
import functools

import jax
import jax.numpy as jnp
from jax import lax
from jax.experimental import pallas as pl
from jax.experimental.pallas import tpu as pltpu
from jax.sharding import PartitionSpec as P

MESH = pl.DeviceIdType.MESH
F32 = jnp.float32
BF16 = jnp.bfloat16
LANES = 128
HALF = 256
PAD = 8


def dot(a, b):
    return jnp.dot(a, b, preferred_element_type=F32)


def twice(block):
    return jnp.concatenate([block, block], axis=1)


def tile_of(rows, most, unit):
    tile = unit
    for size in range(unit, most + 1, unit):
        if rows % size == 0:
            tile = size
    return tile


def kernel(
    plan,
    b_hbm,
    inv_hbm,
    cinv_hbm,
    shift_ref,
    basis_ref,
    count_ref,
    face_ref,
    sol_hbm,
    res_ref,
    bv,
    inv,
    basis_t,
    wide,
    shift_col,
    pick,
    place,
    inv_place,
    acc,
    local,
    prio,
    zpad,
    zb,
    ubuf,
    ub16,
    fsend,
    frecv,
    zq,
    zbq,
    yq,
    uq,
    fsend_q,
    frecv_q,
    cpart,
    coef,
    cg,
    cpsend,
    cprecv,
    co,
    rb1,
    rb2,
    weights,
    ssem,
    rsem,
    lsem,
):
    nz, nx, ny = plan
    nj = 2 * nx
    subs = nz * nj
    kmax, n = basis_ref.shape
    cells = n // 3
    nq = n // ny
    hq = nq // 2
    face = face_ref.shape[1]
    faces = 2 * face

    me_s = lax.axis_index("sub")
    me_y = lax.axis_index("crs")
    j = lax.rem(me_s, nj)
    z = me_s // nj
    my_half = me_y // 2
    my_side = lax.rem(me_y, 2)

    def at_y(k):
        return (me_s, lax.rem(me_y + k, ny))

    def at_z(k):
        return (lax.rem(z + k, nz) * nj + j, me_y)

    def at_j(k):
        return (z * nj + lax.rem(j + k, nj), me_y)

    above = (lax.rem(me_s + 1, subs), me_y)
    below = (lax.rem(me_s + subs - 1, subs), me_y)

    def side(block):
        return jnp.where(my_side == 0, block[:, :LANES], block[:, LANES:])

    used = [0]
    sent = []

    def describe(i, src, dst, device):
        return pltpu.make_async_remote_copy(
            src_ref=src,
            dst_ref=dst,
            send_sem=ssem.at[i],
            recv_sem=rsem.at[i],
            device_id=device,
            device_id_type=MESH,
        )

    def remote(src, dst, device, slot):
        i = used[0]
        used[0] += 1
        cp = describe(i, src, dst, device)
        cp.start()
        sent.append(cp)
        arrived = describe(i, slot, slot, device)
        return arrived

    def wait_all(waits):
        for w in waits:
            w.wait_recv()

    ext = nq + kmax
    cut = ext // 2
    tiles = ((0, cut), (cut, ext - cut))

    def load_b(h):
        return pltpu.make_async_copy(b_hbm.at[:, pl.ds(h * HALF, HALF)], bv.at[h], lsem.at[h])

    def load_inv(i):
        rows = pl.ds(tiles[i][0], min(tiles[i][1], nq - tiles[i][0]))
        return pltpu.make_async_copy(inv_hbm.at[rows, :], inv.at[rows, :], lsem.at[2 + i])

    loads = [load_b(0), load_inv(0), load_inv(1), load_b(1)]
    for cp in loads:
        cp.start()

    barrier = pltpu.get_barrier_semaphore()
    partners = [at_y(k) for k in range(1, ny)] + [at_z(k) for k in range(1, nz)]
    partners += [at_j(k) for k in range(1, nj)] + [above, below]
    for device in partners:
        pl.semaphore_signal(barrier, inc=1, device_id=device, device_id_type=MESH)

    keep = lax.broadcasted_iota(jnp.int32, (kmax, n), 0) < count_ref[0]
    masked = jnp.where(keep, basis_ref[...].astype(F32), 0.0)
    inv[pl.ds(nq, kmax), :] = masked.astype(BF16)
    wide[...] = jnp.zeros_like(wide)
    wide[pl.ds(0, kmax), :] = masked

    pl.semaphore_wait(barrier, len(partners))

    mine_z = cinv_hbm.shape[0]
    part_sem = used[0]
    used[0] += ny - 1
    wanted = cinv_hbm.at[:, j, :, pl.ds(pl.multiple_of(z * nj * kmax, nj * kmax), nj * kmax)]

    def part_slot(k):
        return cpart.at[pl.ds(lax.rem(me_y + k, ny) * mine_z, mine_z)]

    own_part_copy = pltpu.make_async_copy(wanted, part_slot(0), lsem.at[4])
    own_part_copy.start()

    def part_begin():
        for k in range(1, ny):
            describe(part_sem + k - 1, wanted, part_slot(0), at_y(k)).start()

    def part_end():
        own_part_copy.wait()
        for k in range(1, ny):
            describe(part_sem + k - 1, wanted, part_slot(0), at_y(k)).wait_send()
            slot = part_slot(ny - k)
            describe(part_sem + k - 1, slot, slot, at_y(k)).wait_recv()

    def coarse_begin(it):
        cg[it, j] = side(coef[it, my_half]).astype(BF16)
        mine = cg.at[it, j]
        return [
            remote(mine, mine, at_j(k), cg.at[it, lax.rem(j + nj - k, nj)]) for k in range(1, nj)
        ]

    def coarse_line(it, waits):
        wait_all(waits)
        rows = cpart[...].reshape(nz * kmax, nj * kmax)
        partial = dot(rows, cg[it].reshape(nj * kmax, LANES))
        cpsend[it] = partial.reshape(nz, kmax, LANES)
        cprecv[it, z] = cpsend[it, z]
        return [
            remote(
                cpsend.at[it, lax.rem(z + k, nz)],
                cprecv.at[it, z],
                at_z(k),
                cprecv.at[it, lax.rem(z + nz - k, nz)],
            )
            for k in range(1, nz)
        ]

    def coarse_end(it, waits):
        wait_all(waits)
        co[it, me_y] = jnp.sum(cprecv[it], axis=0).astype(BF16)
        mine = co.at[it, me_y]
        return [
            remote(mine, mine, at_y(k), co.at[it, lax.rem(me_y + ny - k, ny)])
            for k in range(1, ny)
        ]

    base = pl.multiple_of(me_y * nq, nq)
    right, left = at_y(1), at_y(ny - 1)

    def part_rows(k, low):
        owner_y = lax.rem(me_y + k, ny)
        return pl.ds(pl.multiple_of(owner_y * nq + (0 if low else hq), hq), hq)

    def keep_product(it, h, start, size, out):
        rows = min(size, nq - start)
        local[it, h, pl.ds(pl.multiple_of(base + start, 16), rows), :] = out[:rows].astype(BF16)
        if rows < size:
            coef[it, h] = out[rows:]

    def first_product(h, ready=None):
        for i, (start, size) in enumerate(tiles):
            if ready is not None:
                ready(i)
            keep_product(0, h, start, size, dot(inv[pl.ds(start, size), :], bv[h]))

    def second_product(h):
        for start, size in tiles:
            acc[pl.ds(start, size), :] = dot(inv[pl.ds(start, size), :], ub16[...])

    def second_faces(h, waits):
        wait_all(waits)
        for start, size in tiles:
            rows = pl.ds(start, size)
            out = acc[rows, :] - 4.0 * dot(inv_place[rows, :], frecv[h])
            keep_product(1, h, start, size, out)

    def gather_begin(it, h, first):
        buf = local.at[it, h]

        def send(k, low, device):
            mine = buf.at[part_rows(0, low), :]
            return remote(mine, mine, device, buf.at[part_rows(k, low), :])

        if first:
            return send(ny - 1, True, right), send(1, False, left)
        return send(ny - 1, False, right), send(1, True, left)

    def gather_forward(it, h, waits):
        buf = local.at[it, h]
        waits[0].wait_recv()
        low = buf.at[part_rows(ny - 1, True), :]
        far_low = remote(low, low, right, buf.at[part_rows(2, True), :])
        waits[1].wait_recv()
        high = buf.at[part_rows(1, False), :]
        far_high = remote(high, high, left, buf.at[part_rows(2, False), :])
        return far_low, far_high

    def padded(block):
        rest = jnp.zeros((LANES - kmax, block.shape[1]), BF16)
        return jnp.concatenate([block, rest], axis=0)

    def coarse_half(it, h):
        return padded(jnp.concatenate([co[it, 2 * h], co[it, 2 * h + 1]], axis=1))

    def assemble(h):
        coarse = coarse_half(0, h)
        tile = tile_of(cells, 768, 16)
        per = cells // tile

        @pl.loop(0, 3 * per)
        def _(i):
            comp = i // per
            rows = pl.ds(pl.multiple_of(i * tile, tile), tile)
            value = local[0, h, rows, :].astype(F32) + dot(basis_t[rows, :], coarse)
            start = pl.multiple_of(lax.rem(i, per) * tile + PAD, PAD)
            zpad[h, comp, pl.ds(start, tile), :] = value
            zb[rows, :] = value.astype(BF16)

    def assemble_quarter(field):
        coarse = padded(co[1, me_y])
        tile = tile_of(cells, 768, 16)
        per = cells // tile

        @pl.loop(0, 3 * per)
        def _(i):
            comp = i // per
            rows = pl.ds(pl.multiple_of(i * tile, tile), tile)
            value = field(rows).astype(F32) + dot(basis_t[rows, :], coarse)
            start = pl.multiple_of(lax.rem(i, per) * tile + PAD, PAD)
            zq[comp, pl.ds(start, tile), :] = value
            zbq[rows, :] = value.astype(BF16)

    lower, upper = pl.ds(0, face), pl.ds(face, face)

    def faces_begin(field, out, into):
        tile = tile_of(face, 192, 16)
        waits = []
        for start in range(0, face, tile):
            for first, other, device in ((face, 0, above), (0, face, below)):
                rows, there = pl.ds(first + start, tile), pl.ds(other + start, tile)
                out[rows, :] = dot(pick[rows, :], field[...]).astype(BF16)
                waits.append(
                    remote(out.at[rows, :], into.at[there, :], device, into.at[there, :])
                )
        return waits

    def stencil(load, shift_of, store):
        size = tile_of(cells, 32, 16)

        @pl.loop(0, cells // size)
        def _(i):
            m0 = pl.multiple_of(i * size, size)
            blocks = [load(comp, pl.ds(m0, size + 2 * PAD)) for comp in range(3)]
            mid = [block[PAD : PAD + size] for block in blocks]
            total = 0.5 * (mid[0] + mid[1] + mid[2])
            for comp in range(3):
                rows = pl.ds(pl.multiple_of(comp * cells + m0, size), size)
                value = (6.5 + shift_of(rows)) * mid[comp] - total
                value -= blocks[comp][PAD - 1 : PAD - 1 + size]
                value -= blocks[comp][PAD + 1 : PAD + 1 + size]
                store(rows, value)

    def stencil_half(h):
        def store(rows, value):
            ubuf[h, rows, :] = value
            ub16[rows, :] = value.astype(BF16)

        stencil(lambda c, r: zpad[h, c, r, :], lambda r: twice(shift_col[r, :]), store)

    def stencil_quarter():
        def store(rows, value):
            yq[rows, :] = value

        stencil(lambda c, r: zq[c, r, :], lambda r: shift_col[r, :], store)

    def prepare(h):
        coarse = coarse_half(1, h)
        tile = tile_of(n, 768, 16)

        @pl.loop(0, n // tile)
        def _(i):
            rows = pl.ds(pl.multiple_of(i * tile, tile), tile)
            ubuf[h, rows, :] = local[1, h, rows, :].astype(F32) + dot(basis_t[rows, :], coarse)

    def fold(value):
        return jnp.sum(value.reshape(value.shape[0] // 8, 8, LANES), axis=0)

    def inner_products(terms):
        tile = tile_of(n, 768, 16)

        def step(i, sums):
            rows = pl.ds(pl.multiple_of(i * tile, tile), tile)
            return tuple(s + fold(t) for s, t in zip(sums, terms(rows)))

        zero = jnp.zeros((8, LANES), F32)
        sums = lax.fori_loop(0, n // tile, step, (zero, zero, zero))
        rows = [jnp.sum(value, axis=0, keepdims=True) for value in sums]
        return jnp.concatenate(rows + [jnp.zeros((5, LANES), F32)], axis=0)

    def first_terms(rows):
        b = side(bv[my_half, rows, :]).astype(F32)
        u = side(ubuf[my_half, rows, :] - 4.0 * dot(place[rows, :], frecv[my_half]))
        uq[rows, :] = u
        return b * b, u * b, u * u

    def second_terms(h11, rows):
        b = side(bv[my_half, rows, :]).astype(F32)
        u = uq[rows, :]
        g = yq[rows, :] - 4.0 * dot(place[rows, :], frecv_q[...]) - h11 * u
        t = u - h11 * b
        return g * b, g * t, g * g

    def reduce_begin(it, partial):
        rb1[it, j] = partial
        mine = rb1.at[it, j]
        return [
            remote(mine, mine, at_j(k), rb1.at[it, lax.rem(j + nj - k, nj)]) for k in range(1, nj)
        ]

    def reduce_z(it, waits):
        wait_all(waits)
        rb2[it, z] = jnp.sum(rb1[it], axis=0)
        mine = rb2.at[it, z]
        return [
            remote(mine, mine, at_z(k), rb2.at[it, lax.rem(z + nz - k, nz)]) for k in range(1, nz)
        ]

    def reduce_end(it, waits):
        wait_all(waits)
        total = jnp.sum(rb2[it], axis=0)
        return total[0:1], total[1:2], total[2:3]

    def build_pads():
        for i in range(n // LANES):
            block = wide[:, i * LANES : (i + 1) * LANES]
            basis_t[pl.ds(i * LANES, LANES), :] = block.T.astype(BF16)
        for h in range(2):
            for comp in range(3):
                for start in (0, cells + PAD):
                    zpad[h, comp, pl.ds(start, PAD), :] = jnp.zeros((PAD, HALF), F32)
        for comp in range(3):
            for start in (0, cells + PAD):
                zq[comp, pl.ds(start, PAD), :] = jnp.zeros((PAD, LANES), F32)
        for i in range(n // LANES):
            row = jnp.broadcast_to(shift_ref[:, i * LANES : (i + 1) * LANES], (LANES, LANES))
            shift_col[pl.ds(i * LANES, LANES), :] = row.T

    lane = lax.broadcasted_iota(jnp.int32, (LANES, LANES), 1)
    line = lax.broadcasted_iota(jnp.int32, (LANES, LANES), 0)

    face_all = jnp.concatenate([face_ref[0:1, :], face_ref[1:2, :]], axis=1)

    def face_row(i):
        return jnp.broadcast_to(face_all[:, i * LANES : (i + 1) * LANES], (LANES, LANES))

    def build_pick():
        for i in range(faces // LANES):
            column = face_row(i).astype(F32).T.astype(jnp.int32)
            for k in range(n // LANES):
                hit = jnp.where(column == lane + k * LANES, 1.0, 0.0)
                pick[pl.ds(i * LANES, LANES), k * LANES : (k + 1) * LANES] = hit.astype(BF16)

    def build_place():
        for i in range(faces // LANES):
            slot = lane + i * LANES
            missing = ((slot < face) & (me_s == 0)) | ((slot >= face) & (me_s == subs - 1))
            row = jnp.where(missing, -1, face_row(i))
            for k in range(n // LANES):
                hit = jnp.where(row == line + k * LANES, 1.0, 0.0)
                place[pl.ds(k * LANES, LANES), i * LANES : (i + 1) * LANES] = hit.astype(BF16)

    def build_inv_place():
        for start, size in tiles:
            rows = pl.ds(start, size)
            width = tile_of(faces, 384, LANES)

            @pl.loop(0, faces // width)
            def _(i):
                cols = pl.ds(pl.multiple_of(i * width, width), width)
                inv_place[rows, cols] = dot(inv[rows, :], place[:, cols]).astype(BF16)

    def ready(i):
        if i == 0:
            loads[0].wait()
        loads[1 + i].wait()

    part_begin()
    first_product(0, ready)
    g00 = gather_begin(0, 0, True)
    loads[3].wait()
    first_product(1)
    coarse = coarse_begin(0)
    build_pads()
    g00_near = gather_begin(0, 0, False)
    build_pick()
    g00 = gather_forward(0, 0, g00)
    build_place()
    part_end()
    coarse = coarse_line(0, coarse)
    build_inv_place()
    wait_all(g00_near)
    g01 = gather_begin(0, 1, True)
    coarse = coarse_end(0, coarse)
    wait_all(g00)
    wait_all(coarse)
    assemble(0)
    g01_near = gather_begin(0, 1, False)
    f00 = faces_begin(zb, fsend.at[0], frecv.at[0])
    stencil_half(0)
    g01 = gather_forward(0, 1, g01)

    second_product(0)
    second_faces(0, f00)
    g10 = gather_begin(1, 0, True)
    wait_all(g01_near)
    wait_all(g01)
    assemble(1)
    f01 = faces_begin(zb, fsend.at[1], frecv.at[1])
    g10_near = gather_begin(1, 0, False)
    stencil_half(1)
    second_product(1)
    g10 = gather_forward(1, 0, g10)
    second_faces(1, f01)
    coarse = coarse_begin(1)

    prio_sem = used[0]
    used[0] += ny - 1
    own_part = pl.ds(base, nq)

    def prio_copy(k):
        target = lax.rem(me_y + k, ny)
        col = pl.multiple_of(lax.rem(target, 2) * LANES, LANES)
        return target, describe(
            prio_sem + k - 1,
            local.at[1, 1, own_part, pl.ds(col, LANES)],
            prio.at[own_part, :],
            at_y(k),
        )

    def prio_begin():
        for k in range(1, ny):
            target, cp = prio_copy(k)

            @pl.when(target // 2 == 1)
            def _(cp=cp):
                cp.start()

        @pl.when(my_half == 1)
        def _():
            prio[own_part, :] = side(local[1, 1, own_part, :].astype(F32)).astype(BF16)

    def prio_end():
        for k in range(1, ny):
            target, cp = prio_copy(k)

            @pl.when(target // 2 == 1)
            def _(cp=cp):
                cp.wait_send()

        @pl.when(my_half == 1)
        def _():
            for k in range(1, ny):
                source = lax.rem(me_y + ny - k, ny)
                slot = prio.at[pl.ds(pl.multiple_of(source * nq, nq), nq), :]
                describe(prio_sem + k - 1, slot, slot, at_y(k)).wait_recv()

    prio_begin()
    r0 = reduce_begin(0, inner_products(first_terms))
    coarse = coarse_line(1, coarse)
    g11 = gather_begin(1, 1, True)
    r0 = reduce_z(0, r0)
    g11_near = gather_begin(1, 1, False)
    coarse = coarse_end(1, coarse)
    prio_end()
    wait_all(g10_near)
    wait_all(g10)

    @pl.when(my_half == 0)
    def _():
        assemble_quarter(lambda rows: side(local[1, 0, rows, :].astype(F32)))

    @pl.when(my_half == 1)
    def _():
        assemble_quarter(lambda rows: prio[rows, :])

    f1 = faces_begin(zbq, fsend_q, frecv_q)
    g11 = gather_forward(1, 1, g11)
    bb, ub, uu = reduce_end(0, r0)
    stencil_quarter()
    beta2 = bb + 1e-12
    beta = jnp.sqrt(beta2)
    h11 = ub / beta2
    h21s = jnp.maximum((uu - h11 * (2.0 * ub - h11 * bb)) / beta2, 0.0) + 1e-12
    h21 = jnp.sqrt(h21s)
    wait_all(f1)
    r1 = reduce_begin(1, inner_products(functools.partial(second_terms, h11)))
    wait_all(coarse)
    prepare(0)
    r1 = reduce_z(1, r1)
    wait_all(g11_near)
    wait_all(g11)
    prepare(1)
    gb, gt, gg = reduce_end(1, r1)

    scale = 1.0 / (beta * h21)
    h12 = gb * scale / beta
    h22 = gt * scale * scale
    ww = gg * scale * scale
    ff_gap = 1e-12 / beta2
    ss_gap = 1e-12 / h21s
    fs = h11 * ff_gap / h21
    h32s = ww - h12 * h12 * (1.0 + ff_gap) - h22 * h22 * (1.0 + ss_gap) + 2.0 * h12 * h22 * fs
    h32 = jnp.sqrt(jnp.maximum(h32s, 0.0) + 1e-12)
    dist_one = jnp.sqrt(h11 * h11 + h21 * h21)
    cos_one = h11 / dist_one
    sin_one = h21 / dist_one
    r12 = cos_one * h12 + sin_one * h22
    t22 = cos_one * h22 - sin_one * h12
    dist_two = jnp.sqrt(t22 * t22 + h32 * h32)
    cos_two = t22 / dist_two
    sin_two = h32 / dist_two
    y2 = -cos_two * sin_one * beta / dist_two
    y1 = (cos_one * beta - r12 * y2) / dist_one
    weight_two = y2 * scale
    weight_one = y1 / beta - h11 * weight_two
    residual = jnp.abs(sin_one * sin_two)
    weights[me_y] = jnp.concatenate(
        [weight_one, weight_two, residual, jnp.zeros((5, LANES), F32)], axis=0
    )
    mine = weights.at[me_y]
    w1 = [
        remote(mine, mine, at_y(k), weights.at[lax.rem(me_y + ny - k, ny)]) for k in range(1, ny)
    ]

    def finish(h):
        def pair(i):
            return jnp.concatenate([weights[2 * h, i : i + 1], weights[2 * h + 1, i : i + 1]], axis=1)

        one_w, two_w, res = pair(0), pair(1), pair(2)
        res_ref[:, h * HALF : (h + 1) * HALF] = res
        tile = tile_of(cells, 256, 16)
        outs = []
        for comp in range(3):

            @pl.loop(0, cells // tile)
            def _(i, comp=comp):
                m0 = pl.multiple_of(i * tile, tile)
                rows = pl.ds(pl.multiple_of(comp * cells + m0, tile), tile)
                one = zpad[h, comp, pl.ds(m0 + PAD, tile), :]
                bv[h, rows, :] = (one * one_w + ubuf[h, rows, :] * two_w).astype(BF16)

            rows = pl.ds(comp * cells, cells)
            out = pltpu.make_async_copy(
                bv.at[h, rows, :],
                sol_hbm.at[rows, pl.ds(h * HALF, HALF)],
                lsem.at[5 + 3 * h + comp],
            )
            out.start()
            outs.append(out)
        return outs

    wait_all(w1)
    outs = finish(0)
    outs += finish(1)
    for cp in sent:
        cp.wait_send()
    for cp in outs:
        cp.wait()
    assert used[0] <= ssem.shape[0]


def count_copies(nz, nx, ny, rims):
    line, group = nz - 1, 2 * nx - 1
    coarse = 2 * (line + group + ny - 1)
    return 3 * (ny - 1) + coarse + 4 * 6 + 3 * rims + 2 * (group + line)


def per_device(nz, nx, right_sides, shift, inverses, basis, counts, face_rows, coarse_inverse):
    ny = lax.axis_size("crs")
    n, width = right_sides.shape[1:]
    nq = n // ny
    kmax = basis.shape[1]
    faces = 2 * face_rows.shape[2]
    cells = n // 3
    nj = 2 * nx
    subs = nz * nj
    ext = nq + kmax
    copies = count_copies(nz, nx, ny, 2 * (faces // 2 // tile_of(faces // 2, 192, 16)))
    any_spec = pl.BlockSpec(memory_space=pl.ANY)
    vmem = pl.BlockSpec(memory_space=pltpu.VMEM)
    out, residual = pl.pallas_call(
        functools.partial(kernel, (nz, nx, ny)),
        out_shape=(
            jax.ShapeDtypeStruct((n, width), BF16),
            jax.ShapeDtypeStruct((1, width), F32),
        ),
        in_specs=[
            any_spec,
            any_spec,
            any_spec,
            vmem,
            vmem,
            pl.BlockSpec(memory_space=pltpu.SMEM),
            vmem,
        ],
        out_specs=(any_spec, vmem),
        scratch_shapes=[
            pltpu.VMEM((2, n, HALF), BF16),
            pltpu.VMEM((ext, n), BF16),
            pltpu.VMEM((n, LANES), BF16),
            pltpu.VMEM((LANES, n), F32),
            pltpu.VMEM((n, LANES), F32),
            pltpu.VMEM((faces, n), BF16),
            pltpu.VMEM((n, faces), BF16),
            pltpu.VMEM((ext, faces), BF16),
            pltpu.VMEM((ext, HALF), F32),
            pltpu.VMEM((2, 2, n, HALF), BF16),
            pltpu.VMEM((n, LANES), BF16),
            pltpu.VMEM((2, 3, cells + 2 * PAD, HALF), F32),
            pltpu.VMEM((n, HALF), BF16),
            pltpu.VMEM((2, n, HALF), F32),
            pltpu.VMEM((n, HALF), BF16),
            pltpu.VMEM((2, faces, HALF), BF16),
            pltpu.VMEM((2, faces, HALF), BF16),
            pltpu.VMEM((3, cells + 2 * PAD, LANES), F32),
            pltpu.VMEM((n, LANES), BF16),
            pltpu.VMEM((n, LANES), F32),
            pltpu.VMEM((n, LANES), F32),
            pltpu.VMEM((faces, LANES), BF16),
            pltpu.VMEM((faces, LANES), BF16),
            pltpu.VMEM((nz, kmax, nj * kmax), BF16),
            pltpu.VMEM((2, 2, kmax, HALF), F32),
            pltpu.VMEM((2, nj, kmax, LANES), BF16),
            pltpu.VMEM((2, nz, kmax, LANES), F32),
            pltpu.VMEM((2, nz, kmax, LANES), F32),
            pltpu.VMEM((2, ny, kmax, LANES), BF16),
            pltpu.VMEM((2, nj, 8, LANES), F32),
            pltpu.VMEM((2, nz, 8, LANES), F32),
            pltpu.VMEM((ny, 8, LANES), F32),
            pltpu.SemaphoreType.DMA((copies,)),
            pltpu.SemaphoreType.DMA((copies,)),
            pltpu.SemaphoreType.DMA((11,)),
        ],
        compiler_params=pltpu.CompilerParams(
            collective_id=0, has_side_effects=True, vmem_limit_bytes=60 * 1024 * 1024
        ),
    )(
        right_sides[0],
        inverses[0],
        coarse_inverse.reshape(-1, nj, kmax, subs * kmax),
        shift,
        basis[0],
        counts,
        face_rows[0],
    )
    return out[None], residual.reshape(width)


def solution(mesh):
    subs = mesh.shape["sub"]
    nz = 8 if subs == 64 else subs // 2
    nx = subs // (2 * nz)
    return jax.shard_map(
        functools.partial(per_device, nz, nx),
        mesh=mesh,
        in_specs=(
            P("sub", None, None),
            P("sub", None),
            P("sub", "crs", None),
            P("sub", None, None),
            P("sub"),
            P("sub", None, None),
            P("crs", None),
        ),
        out_specs=(P("sub", None, None), P()),
        check_vma=False,
    )
```
